512 devices in a mesh: dp: 64 (over z, x), group: 8 (over y, core).
Axes of the slice: x: 4, y: 4, z: 16, core: 2. Of those that a mesh axis runs over, the one named last changes fastest.
Arguments:
- query_hidden: bfloat16 [4096, 4096], P(('dp', 'group')), may hold values from -0.2 to 0.2
- passage_hidden: bfloat16 [16384, 4096], P(('dp', 'group')), may hold values from -0.2 to 0.2
- projection: bfloat16 [4096, 4096], P(None, 'group'), may hold values from -0.09375 to 0.09375
- negative_ids: int32 [4096, 16], replicated, may hold values from 0 to 16383, as said below
Outputs:
- query_loss: float32 [4096], P(('dp', 'group'))
- query_hidden_grad: bfloat16 [4096, 4096], P(('dp', 'group'))
- passage_hidden_grad: bfloat16 [16384, 4096], P(('dp', 'group'))
The draws below stay inside these ranges and needn't reach their ends.
Inputs may be any that keep to these rules, and one draw needn't show every extreme that they name: `negative_ids`: take the 64 queries of one index of dp, rows a * 64 to (a + 1) * 64 - 1. Of their 1024 ids, at most 32 name passages of any one index o of dp (ids o * 256 to (o + 1) * 256 - 1), and some index of dp receives exactly 32 from every index of dp.
All inputs are finite; a program needn't handle non-finite values.
Results may differ from the reference program's by a relative error of at most 0.017.
Values may be sent and summed in bfloat16 or wider, within the bound.
A program may use at most 64 MiB of HBM per device.

```python
import jax
import jax.numpy as jnp
from jax import lax

D = 4096
PPQ = 4
NEG = 16
NQ = 4096
NP = 16384
NGQ = 64
NGP = 256
REQ = 1024
CAP = 32
N_DP = 64
N_GROUP = 8


VALUE_LIMIT = 0.19921875


def topic_layout(key):
    topic_count = min(64, NGP)
    layout_key = jax.random.fold_in(key, 700)
    query_key, order_key = jax.random.split(layout_key)
    query_topic = jax.random.randint(query_key, (NQ,), 0, topic_count, dtype=jnp.int32)
    owner_keys = jax.random.split(order_key, N_DP)
    orders = jax.vmap(lambda owner_key: jax.random.permutation(owner_key, NGP).astype(jnp.int32))(owner_keys)
    return (topic_count, query_topic, orders)


def topic_vectors(key, topic_count):
    vector_key = jax.random.fold_in(key, 800)
    return jnp.clip(jax.random.normal(vector_key, (topic_count, D), jnp.float32), -4.0, 4.0)


def query_base(key):
    base_key = jax.random.fold_in(key, 500)
    return jnp.clip(jax.random.normal(base_key, (NQ, D), jnp.float32), -4.0, 4.0)


def draw_query_hidden(key, part):
    topic_count, query_topic, orders = topic_layout(key)
    vectors = topic_vectors(key, topic_count)
    mixed = 0.75 * query_base(key) + 0.66 * jnp.take(vectors, query_topic, axis=0)
    values = mixed
    return jnp.clip(0.02 * values, -VALUE_LIMIT, VALUE_LIMIT).astype(jnp.bfloat16)


def draw_passage_hidden(key, part):
    topic_count, query_topic, orders = topic_layout(key)
    vectors = topic_vectors(key, topic_count)
    passage_topic = (orders % topic_count).reshape(NP)
    anchor = query_base(key)
    key = jax.random.fold_in(key, 2)
    noise_key = jax.random.fold_in(key, 0)
    strength_key = jax.random.fold_in(key, 2)
    noise = jnp.clip(jax.random.normal(noise_key, (NQ, PPQ, D), jnp.float32), -4.0, 4.0)
    leading = 0.92 * noise[:, :1] + 0.39 * anchor[:, None, :]
    own_part = jnp.concatenate([leading, noise[:, 1:]], axis=1).reshape(NP, D)
    strength = jax.random.uniform(strength_key, (NP, 1), jnp.float32, 0.4, 0.55)
    mixed = jnp.sqrt(1.0 - strength * strength) * own_part + strength * jnp.take(vectors, passage_topic, axis=0)
    return jnp.clip(0.02 * mixed, -VALUE_LIMIT, VALUE_LIMIT).astype(jnp.bfloat16)


def draw_negative_ids(key, part):
    topic_count, query_topic, orders = topic_layout(key)
    inverse = jnp.argsort(orders, axis=1, stable=True).astype(jnp.int32)
    key = jax.random.fold_in(key, 3)
    rank_key, group_key = jax.random.split(key)
    ranked_owners = jax.random.permutation(rank_key, N_DP).astype(jnp.int32)
    hot_count = N_DP // 4
    cold_count = N_DP - hot_count
    remaining = REQ - hot_count * CAP
    hot_ranks = jnp.repeat(jnp.arange(hot_count, dtype=jnp.int32), CAP)
    per_topic = NGP // topic_count

    def one_group(member_key, group_index):
        slot_key, order_key, pick_key = jax.random.split(member_key, 3)
        chosen = jax.random.permutation(slot_key, cold_count * CAP).astype(jnp.int32)[:remaining]
        rank_list = jnp.concatenate([hot_ranks, hot_count + chosen // CAP])
        rank_list = jax.random.permutation(order_key, rank_list)
        owners = ranked_owners[rank_list]
        pick_draws = jax.random.randint(pick_key, (3, REQ), 0, per_topic, dtype=jnp.int32)
        within_topic = jnp.min(pick_draws, axis=0)
        asking_query = group_index * NGQ + jnp.arange(REQ, dtype=jnp.int32) // NEG
        wanted_topic = query_topic[asking_query]
        local_index = inverse[owners, wanted_topic + topic_count * within_topic]
        return owners * NGP + local_index
    all_ids = jax.vmap(one_group)(jax.random.split(group_key, N_DP), jnp.arange(N_DP, dtype=jnp.int32))
    return all_ids.reshape(NQ, NEG).astype(jnp.int32)


def block_scale(stream_key, shape, pieces, low, high):
    def one(position, shards_of):
        draws = jax.random.uniform(jax.random.fold_in(jax.random.fold_in(stream_key, 6), position), (shards_of,), jnp.float32, low / len(pieces), high / len(pieces))
        return jnp.repeat(jnp.exp(draws), shape[position] // shards_of).reshape((-1,) + (1,) * (len(shape) - position - 1))

    gain = one(*pieces[0])
    for cut in pieces[1:]:
        gain = gain * one(*cut)
    return gain


def bell_draw(key, dims, width, limit, cuts=(), kind=jnp.bfloat16):
    array = jax.random.normal(key, dims, jnp.float32) * width
    if len(cuts) > 0:
        array = block_scale(key, dims, cuts, -0.22, 0.18) * array
    return jnp.clip(array, min=-limit, max=limit).astype(kind)


def setup_inputs(seed: int = 0) -> dict:
    arg_keys = jax.random.split(jax.random.key(seed), 5)
    return {
        "query_hidden": draw_query_hidden(jax.random.fold_in(arg_keys[4], 71), 0),
        "passage_hidden": draw_passage_hidden(jax.random.fold_in(arg_keys[4], 71), 0),
        "projection": bell_draw(arg_keys[2], (D, D), D ** -0.5, 0.09375, ((1, 8),)),
        "negative_ids": draw_negative_ids(jax.random.fold_in(arg_keys[4], 71), 0),
    }


SOFTMAX_TEMP_SCALE = 0.05
EPSILON = 1e-06

def hidden_grads(down_rows, projection):
    block_width = D // N_GROUP
    result = jnp.zeros((down_rows.shape[0], D), jnp.float32)
    for block_index in range(N_GROUP):
        column_start = block_index * block_width
        part_down = lax.slice_in_dim(down_rows, column_start, column_start + block_width, axis=1)
        part_weight = lax.slice_in_dim(projection, column_start, column_start + block_width, axis=1)
        partial_term = lax.dot_general(part_down, part_weight, (((1,), (1,)), ((), ())), preferred_element_type=jnp.float32)
        rounded_term = lax.optimization_barrier(partial_term.astype(jnp.bfloat16))
        result = result + rounded_term.astype(jnp.float32)
    return result.astype(jnp.bfloat16)

def reference(query_hidden, passage_hidden, projection, negative_ids):
    proj_query = jnp.dot(query_hidden, projection, preferred_element_type=jnp.float32).astype(jnp.bfloat16)
    proj_passage = jnp.dot(passage_hidden, projection, preferred_element_type=jnp.float32).astype(jnp.bfloat16)
    square_query = lax.optimization_barrier(jnp.sum(jnp.square(proj_query.astype(jnp.float32)), axis=1))
    square_passage = lax.optimization_barrier(jnp.sum(jnp.square(proj_passage.astype(jnp.float32)), axis=1))
    norm_query = jnp.sqrt(square_query + EPSILON)
    norm_passage = jnp.sqrt(square_passage + EPSILON)
    positive_passage = (jnp.arange(NGP, dtype=jnp.int32)[None, :] == (jnp.arange(NGQ, dtype=jnp.int32) * PPQ)[:, None]).astype(jnp.float32)

    def one_group(carried, group_index):
        rows_neg, radial_neg = carried
        query_start = (group_index * NGQ).astype(jnp.int32)
        passage_start = (group_index * NGP).astype(jnp.int32)
        group_query = lax.dynamic_slice_in_dim(proj_query, query_start, NGQ, 0)
        group_passage = lax.dynamic_slice_in_dim(proj_passage, passage_start, NGP, 0)
        group_norm_query = lax.dynamic_slice_in_dim(norm_query, query_start, NGQ, 0)
        group_square_query = lax.dynamic_slice_in_dim(square_query, query_start, NGQ, 0)
        group_norm_passage = lax.dynamic_slice_in_dim(norm_passage, passage_start, NGP, 0)
        group_ids = lax.dynamic_slice_in_dim(negative_ids, query_start, NGQ, 0)
        neg_rows = jnp.take(proj_passage, group_ids, axis=0)
        norm_neg = jnp.take(norm_passage, group_ids, axis=0)
        inner_in = jnp.dot(group_query, group_passage.T, preferred_element_type=jnp.float32)
        inner_neg = jnp.einsum('qd,qkd->qk', group_query.astype(jnp.float32), neg_rows.astype(jnp.float32))
        cosine_positive_pair = inner_in / (group_norm_query[:, None] * group_norm_passage[None, :])
        cosine_negative_pair = inner_neg / (group_norm_query[:, None] * norm_neg)
        positive_weight = jnp.exp((cosine_positive_pair - 1.0) / SOFTMAX_TEMP_SCALE)
        negative_weight = jnp.exp((cosine_negative_pair - 1.0) / SOFTMAX_TEMP_SCALE)
        summed_weight = lax.optimization_barrier(jnp.sum(positive_weight, axis=1)) + lax.optimization_barrier(jnp.sum(negative_weight, axis=1))
        loss_values = jnp.log(summed_weight) + (1.0 - lax.optimization_barrier(jnp.sum(positive_passage * cosine_positive_pair, axis=1))) / SOFTMAX_TEMP_SCALE
        positive_slope = (positive_weight / summed_weight[:, None] - positive_passage) / SOFTMAX_TEMP_SCALE
        negative_slope = negative_weight / summed_weight[:, None] / SOFTMAX_TEMP_SCALE
        radial_query = lax.optimization_barrier(jnp.sum(positive_slope * cosine_positive_pair, axis=1)) + lax.optimization_barrier(jnp.sum(negative_slope * cosine_negative_pair, axis=1))
        radial_in = lax.optimization_barrier(jnp.sum(positive_slope * cosine_positive_pair, axis=0))
        coef_in = (positive_slope / (group_norm_query[:, None] * group_norm_passage[None, :])).astype(jnp.bfloat16)
        coef_neg = (negative_slope / (group_norm_query[:, None] * norm_neg)).astype(jnp.bfloat16)
        grad_query = jnp.dot(coef_in, group_passage, preferred_element_type=jnp.float32) + jnp.einsum('qk,qkd->qd', coef_neg.astype(jnp.float32), neg_rows.astype(jnp.float32)) - (radial_query / (group_square_query + EPSILON))[:, None] * group_query.astype(jnp.float32)
        grad_passage_in = jnp.dot(coef_in.T, group_query, preferred_element_type=jnp.float32)
        flat_ids = group_ids.reshape(NGQ * NEG)
        neg_terms = (coef_neg.astype(jnp.float32)[:, :, None] * group_query.astype(jnp.float32)[:, None, :]).reshape(NGQ * NEG, D)
        rows_neg = rows_neg.at[flat_ids].add(neg_terms)
        radial_neg = radial_neg.at[flat_ids].add((negative_slope * cosine_negative_pair).reshape(NGQ * NEG))
        return ((rows_neg, radial_neg), (loss_values, grad_query, grad_passage_in, radial_in))
    initial = (jnp.zeros((NP, D), jnp.float32), jnp.zeros((NP,), jnp.float32))
    (rows_neg, radial_neg), (loss_values, grad_query, grad_passage_in, radial_in) = lax.scan(one_group, initial, jnp.arange(N_DP, dtype=jnp.int32))
    grad_query = grad_query.reshape(NQ, D)
    radial_passage = radial_in.reshape(NP) + radial_neg
    grad_passage = grad_passage_in.reshape(NP, D) + rows_neg - (radial_passage / (square_passage + EPSILON))[:, None] * proj_passage.astype(jnp.float32)
    query_grad = hidden_grads(grad_query.astype(jnp.bfloat16), projection)
    passage_grad = hidden_grads(grad_passage.astype(jnp.bfloat16), projection)
    return (loss_values.reshape(NQ), query_grad, passage_grad)
```

```python
import jax
import jax.numpy as jnp
from jax import lax
from jax.experimental import pallas as pl
from jax.experimental.pallas import tpu as pltpu
from jax.sharding import PartitionSpec as P

TEMPERATURE = 0.05
EPSILON = 1e-06
MESH = pl.DeviceIdType.MESH
F32, BF16, I32 = jnp.float32, jnp.bfloat16, jnp.int32

NZ, NX, NY, NC = 16, 4, 4, 2
NG = NY * NC
D = 4096
COLS = D // NG
QR, PR, PC = 8, 32, 16
GQ, GP = QR * NG, PR * NG
HALF = GP // 2
NEG, CAP = 16, 32
SLOTS = NX * CAP
CHANNELS = 256
SUBS = 2
SUB = GQ // SUBS


def nn(a, b):
    return lax.dot_general(a, b, (((1,), (0,)), ((), ())), preferred_element_type=F32)


def nt(a, b):
    return lax.dot_general(a, b, (((1,), (1,)), ((), ())), preferred_element_type=F32)


def tn(a, b):
    return lax.dot_general(a, b, (((0,), (0,)), ((), ())), preferred_element_type=F32)


def iota(shape, dim):
    return lax.broadcasted_iota(I32, shape, dim)


def eye(rows, columns):
    return (iota((rows, columns), 0) == iota((rows, columns), 1)).astype(F32)


def to_row(column, identity):
    return jnp.sum(identity * column, axis=0, keepdims=True)


def to_column(row, identity):
    return jnp.sum(identity * row, axis=1, keepdims=True)


def kernel(
    qh, ph, weight_hbm, ids_hbm,
    loss_out, qg_out, pg_out,
    wv, idv, hq, hp, qall, pall, code, hits, one_hot, prow,
    pay1, got1, payn, gotn, nz_out, nz_in, nx_out, nx_in, sl_q, sl_p,
    pay2, got2, sum2, fill, w_p, k_c, r_c, t_out, t_in, inv, r_out, r_in,
    zout, zin, cq, gp, xout, xhalf, xfull,
    qpart, qcore, qout, qfull, ppart, pcore, pout, phalf, pfull,
    local_sem, send_sem, recv_sem,
):
    dp, g = lax.axis_index("dp"), lax.axis_index("group")
    z, x = dp // NX, dp % NX
    y, c = g // NC, g % NC

    def at_z(step):
        return (((z + step + 2 * NZ) % NZ) * NX + x, g)

    def at_x(step):
        return (z * NX + (x + step + NX) % NX, g)

    def member(step, other):
        return ((y + step + NY) % NY) * NC + (1 - c if other else c)

    def at_y(step, other=False):
        return (dp, member(step, other))

    others = [(s, o) for s in (0, 1, 2, 3) for o in (False, True) if (s, o) != (0, False)]

    names, departures = {}, {}

    def channel(name):
        return names.setdefault(name, len(names))

    def copy(name, group, src, dst, device):
        return pltpu.make_async_remote_copy(
            src_ref=src, dst_ref=dst, send_sem=send_sem.at[channel(("from", group))],
            recv_sem=recv_sem.at[channel(name)], device_id=device, device_id_type=MESH,
        )

    def send(name, src, dst, device, group=None):
        group = name if group is None else group
        departures.setdefault(group, None)
        copy(name, group, src, dst, device).start()

    def receive(name, dst):
        if name in departures:
            departures[name] = dst
        copy(name, name, dst, dst, at_x(1)).wait_recv()

    def depart():
        for group, ref in list(departures.items()):
            if ref is not None:
                copy(group, group, ref, ref, at_x(1)).wait_send()
                del departures[group]

    w_copies = []
    for k in range(8):
        rows = pl.ds(k * COLS, COLS)
        w_copies.append(pltpu.make_async_copy(weight_hbm.at[rows], wv.at[rows], local_sem.at[2 + k]))
        w_copies[-1].start()
    id_copy = pltpu.make_async_copy(ids_hbm, idv, local_sem.at[1])
    id_copy.start()
    barrier = pltpu.get_barrier_semaphore()
    greeted = [at_z(s) for s in range(1, NZ)] + [at_x(s) for s in range(1, NX)] + [at_y(*o) for o in others]
    for device in greeted:
        pl.semaphore_signal(barrier, inc=1, device_id=device, device_id_type=MESH)
    pl.semaphore_wait(barrier, len(greeted))

    def columns(h):
        return pl.ds(h * (D // 2), D // 2)

    class Gather:
        def __init__(self, name, src, held):
            self.name, self.src, self.held = name, src, held

        def start(self):
            for k in range(2):
                for sign, step in ((0, 1), (1, -1)):
                    h = k if sign == 0 else 1 - k
                    here = self.held.at[g, :, columns(h)]
                    send((self.name, sign, h), self.src.at[:, columns(h)], here, at_y(step))
            send((self.name, "c"), self.src, self.held.at[g], at_y(0, True))
            self.held[pl.ds(g, 1)] = self.src[...][None]

        def forward(self):
            for k in range(2):
                for sign, step in ((0, 1), (1, -1)):
                    h = k if sign == 0 else 1 - k
                    block = member(-step, False)
                    piece = self.held.at[block, :, columns(h)]
                    receive((self.name, sign, h), piece)
                    if k == 0:
                        send((self.name, "far"), piece, piece, at_y(step))
                    else:
                        whole = self.held.at[block]
                        send((self.name, "c"), whole, whole, at_y(0, True))

        def forward_far(self):
            whole = self.held.at[member(2, False)]
            receive((self.name, "far"), whole)
            send((self.name, "c"), whole, whole, at_y(0, True))

        def finish(self):
            receive((self.name, "c"), self.held.at[pl.ds(0, NY)])

    class Near:
        def __init__(self, name, src, held):
            self.name, self.src, self.held = name, src, held

        def start(self):
            for step in (2, 1, 3):
                send((self.name, step), self.src, self.held.at[g], at_y(step))
            send((self.name, "c"), self.src, self.held.at[g], at_y(0, True))
            self.held[pl.ds(g, 1)] = self.src[...][None]

        def forward(self):
            for step in (1, 3, 2):
                block = self.held.at[member(-step, False)]
                receive((self.name, step), block)
                send((self.name, "c"), block, block, at_y(0, True))

        def finish(self):
            receive((self.name, "c"), self.held.at[pl.ds(0, NY)])

    q_gather = Near("q", qh, hq)
    p_gather = [Gather("p%d" % h, ph.at[pl.ds(h * PC, PC)], hp.at[h]) for h in range(2)]

    last = NZ // 2 - 1

    def halved(sign):
        return range(sign * SUBS // 2, (sign + 1) * SUBS // 2)

    def z_piece(sign, s, j):
        block = (z - (1 - 2 * sign) * s + 2 * NZ) % NZ
        return qall.at[block, pl.ds(j * SUB, SUB)]

    def z_step(s):
        for j in range(SUBS):
            for sign in range(2):
                if s < last or j in halved(sign):
                    piece = z_piece(sign, s, j)
                    if s > 0:
                        receive(("z", sign, s - 1, j), piece)
                    send(("z", sign, s, j), piece, piece, at_z(1 - 2 * sign), "z")

    def z_finish():
        for j in range(SUBS):
            for sign in range(2):
                s = last if j in halved(sign) else last - 1
                receive(("z", sign, s, j), z_piece(sign, s + 1, j))
        departures["z"] = qall.at[pl.ds(0, NZ - 1)]

    def x_piece(block, h, half):
        return pall.at[block, pl.ds(h * HALF + half * (HALF // 2), HALF // 2)]

    def x_start(h):
        for k in range(2):
            for sign in range(2):
                half = k if sign == 0 else 1 - k
                piece = x_piece(x, h, half)
                send(("x", h, sign, half), piece, piece, at_x(1 - 2 * sign))

    def x_forward(h):
        for sign in range(2):
            step = 1 - 2 * sign
            piece = x_piece((x - step + NX) % NX, h, sign)
            receive(("x", h, sign, sign), piece)
            send(("x", h, "far"), piece, piece, at_x(step))

    def x_finish(h):
        for sign in range(2):
            step = 1 - 2 * sign
            receive(("x", h, sign, 1 - sign), x_piece((x - step + NX) % NX, h, 1 - sign))
        receive(("x", h, "far"), pall.at[(x + 2) % NX, pl.ds(h * HALF, HALF)])

    def find_slots():
        pieces = []
        for a in range(NZ):
            start = pl.multiple_of(a * NX * GQ + (x // 2) * 2 * GQ, 2 * GQ)
            pieces.append(idv[:, pl.ds(start, 2 * GQ)].astype(F32))
        turned = jnp.concatenate(pieces, axis=0).T
        odd = (x % 2).astype(F32)
        ids = (turned[:GQ] * (1.0 - odd) + turned[GQ:] * odd).astype(I32)
        owner = (ids >> 8) - z * NX
        place = ids & 255
        place = ((place >> 4) & 1) * HALF + (place >> 5) * PC + (place & 15)
        mine = jnp.concatenate([(owner == o).astype(F32) for o in range(NX)], axis=0)
        picked = mine.astype(BF16)
        shape = (NX * GQ, NZ * NEG)
        i, j = iota(shape, 0), iota(shape, 1)
        before = ((i // GQ == j // GQ) & (j < i)).astype(F32).astype(BF16)
        same = i // NEG == j // NEG
        ahead = (same & (i < j)).astype(F32).astype(BF16)
        row_sums = nn(before, picked).astype(BF16)
        rank = nn(row_sums, same.astype(F32).astype(BF16)) + nn(picked, ahead)
        slot = mine * (rank + ((i // GQ) * CAP + 1).astype(F32))
        slot = slot[:GQ] + slot[GQ : 2 * GQ] + slot[2 * GQ : 3 * GQ] + slot[3 * GQ :]
        both = slot.astype(I32) * 256 + place
        both = jnp.where(slot > 0.0, both, 0)
        for a in range(NZ):
            code[a] = both[:, a * NEG : (a + 1) * NEG]

    def fill_slots(first, count):
        def one(a, carry):
            block = code[a]
            lane = iota((GQ, SLOTS), 1) + 1
            hit = jnp.zeros((GQ, SLOTS), F32)
            spot = jnp.zeros((GQ, SLOTS), I32)
            for k in range(NEG):
                column = jnp.broadcast_to(block[:, k : k + 1], (GQ, SLOTS))
                found = (column >> 8) == lane
                hit = jnp.where(found, 1.0, hit)
                spot = jnp.where(found, column & 255, spot)
            hits[a] = hit
            fill[pl.ds(a, 1), :] = jnp.sum(hit, axis=0, keepdims=True)
            row = jnp.sum(spot.astype(F32), axis=0, keepdims=True)
            column = to_column(row, eye(SLOTS, SLOTS)).astype(I32)
            chosen = (iota((SLOTS, GP), 1) == column).astype(F32).astype(BF16)
            for o in range(NX):
                one_hot[o, a] = chosen[o * CAP : (o + 1) * CAP]
            return carry

        lax.fori_loop(first, first + count, one, 0)

    def share(name, pay, got):
        for step, other in others:
            send(name, pay, got.at[g], at_y(step, other))

    def collect(name, pay, got):
        got[pl.ds(g, 1)] = pay[...][None]
        receive(name, got.at[pl.ds(0, NG - 1)])
        total = got[0]
        for i in range(1, NG):
            total = total + got[i]
        return total

    def project_passages(h):
        rows = hp[h].reshape(HALF, D)
        pall[pl.ds(x, 1), h * HALF : (h + 1) * HALF] = nn(rows, wv[...]).astype(BF16)[None]
        x_start(h)

    eye_q, eye_s = eye(GQ, SLOTS), eye(SLOTS, SLOTS)
    p_first, p_second = p_gather

    q_gather.start()
    id_copy.wait()
    find_slots()
    q_gather.forward()
    p_first.start()
    p_second.start()
    fill_slots(0, 6)
    q_gather.finish()
    rows = hq[...].astype(F32).reshape(GQ, D).astype(BF16)
    projected = jnp.zeros((GQ, COLS), F32)
    for k, one in enumerate(w_copies):
        one.wait()
        part = slice(k * COLS, (k + 1) * COLS)
        projected = projected + nn(rows[:, part], wv[part, :])
    qall[pl.ds(z, 1)] = projected.astype(BF16)[None]
    z_step(0)
    p_first.forward()
    fill_slots(6, 2)
    p_second.forward()
    z_step(1)
    p_first.forward_far()
    fill_slots(8, 2)
    p_first.finish()
    z_step(2)
    project_passages(0)
    p_second.forward_far()
    z_step(3)
    p_second.finish()
    project_passages(1)
    z_step(4)

    own_q, own_p = qall[z], pall[x]
    for h in range(2):
        part = own_p[h * HALF : (h + 1) * HALF]
        payn[h : h + 1] = jnp.sum(nt(part, part) * eye_s, axis=0, keepdims=True)
    own_q32 = own_q.astype(F32)
    payn[2:3] = to_row(jnp.sum(own_q32 * own_q32, axis=1, keepdims=True), eye_q)
    payn[3:] = jnp.zeros((payn.shape[0] - 3, SLOTS), F32)
    share("n", payn, gotn)

    inner = nt(own_q, own_p)
    pay1[0:GQ] = inner[:, :SLOTS]
    pay1[GQ:] = inner[:, SLOTS:]
    share("s1", pay1, got1)
    x_forward(0)
    z_step(5)
    fill_slots(10, 4)
    sums = collect("n", payn, gotn)
    square_p = jnp.concatenate([sums[0:1], sums[1:2]], axis=1)
    square_q = to_column(sums[2:3], eye_q)
    nz_out[...] = sums[2:3]
    nx_out[...] = square_p
    nz_in[pl.ds(z, 1)] = sums[2:3][None]
    nx_in[pl.ds(x, 1)] = square_p[None]
    for s in range(1, NX):
        send("nx", nx_out, nx_in.at[x], at_x(s))
    for s in range(1, NZ):
        send("nz", nz_out, nz_in.at[z], at_z(s))
    x_forward(1)
    z_step(6)
    fill_slots(14, 2)
    x_finish(0)
    z_step(7)
    x_finish(1)

    for o in range(NX):
        chosen = nn(one_hot[o].reshape(NZ * CAP, GP), pall[o])
        prow[:, o * CAP : (o + 1) * CAP, :] = chosen.astype(BF16).reshape(NZ, CAP, COLS)

    def by_groups(one, first=0, count=NZ, width=4):
        def some(i, carry):
            for k in range(width):
                one(first + i * width + k)
            return carry

        lax.fori_loop(0, count // width, some, 0)

    def pair_products(step):
        a = (z + step + 2 * NZ) % NZ
        products = nt(qall[a], prow[a])
        pay2[pl.ds(a, 1), :] = jnp.sum(products * hits[a], axis=0, keepdims=True)

    by_groups(pair_products, 2 - NZ // 2, NZ - 4)
    z_finish()
    for step in (NZ // 2 - 2, NZ // 2 - 1, NZ // 2, NZ // 2 + 1):
        pair_products(step)
    share("s2", pay2, got2)

    receive("nx", nx_in.at[pl.ds(0, NX - 1)])
    receive("nz", nz_in.at[pl.ds(0, NZ - 1)])

    depart()

    def slot_norms(a):
        column = to_column(nz_in[a], eye(GQ, SLOTS))
        sl_q[pl.ds(a, 1), :] = jnp.sum(hits[a] * column, axis=0, keepdims=True)
        columns = [
            jnp.sum(one_hot[o, a].astype(F32) * nx_in[o], axis=1, keepdims=True) for o in range(NX)
        ]
        sl_p[pl.ds(a, 1), :] = to_row(jnp.concatenate(columns, axis=0), eye(SLOTS, SLOTS))

    by_groups(slot_norms)

    sums = collect("s1", pay1, got1)
    inner = jnp.concatenate([sums[0:GQ], sums[GQ : 2 * GQ]], axis=1)
    norm = jnp.sqrt(square_q + EPSILON) * jnp.sqrt(square_p + EPSILON)
    cosine = inner / norm
    weight = jnp.exp((cosine - 1.0) / TEMPERATURE)
    weight_sum = jnp.sum(weight, axis=1, keepdims=True)
    spot = iota((GQ, GP), 1)
    passage = ((spot >> 4) & 7) * PR + (spot >> 7) * PC + (spot & 15)
    positive = (passage == iota((GQ, GP), 0) * 4).astype(F32)

    inner_slot = collect("s2", pay2, got2)
    square_slot_p = sl_p[...]
    norm_slot_q = jnp.sqrt(sl_q[...] + EPSILON)
    norm_slot_p = jnp.sqrt(square_slot_p + EPSILON)
    cosine_slot = inner_slot / (norm_slot_q * norm_slot_p)
    weight_slot = jnp.exp((cosine_slot - 1.0) / TEMPERATURE) * fill[...]
    sum2[0:NZ] = weight_slot
    sum2[NZ:] = weight_slot * cosine_slot
    w_p[...] = weight_slot / norm_slot_p
    k_c[...] = weight_slot / (norm_slot_q * norm_slot_p) / TEMPERATURE
    r_c[...] = weight_slot * cosine_slot / (square_slot_p + EPSILON) / TEMPERATURE

    def query_terms(a):
        coefficient = (hits[a] * w_p[pl.ds(a, 1), :]).astype(BF16)
        return nn(coefficient, prow[a])

    def zr_step(s):
        far = query_terms((z + NZ // 2) % NZ) if s == 0 else None
        terms = []
        for sign, step in ((0, 1), (1, -1)):
            block = (z + step * (NZ // 2 - s) + NZ) % NZ
            terms.append(far if s == 0 else query_terms(block))
        for j in range(SUBS):
            for sign, step in ((0, 1), (1, -1)):
                if s == 0 and j not in halved(sign):
                    continue
                value = terms[sign][j * SUB : (j + 1) * SUB]
                if s > 1 or (s == 1 and j in halved(sign)):
                    receive(("zr", sign, s - 1, j), zin.at[sign, s - 1, j])
                    value = value + zin[sign, s - 1, j].astype(F32)
                zout[sign, s, j] = value.astype(BF16)
                send(("zr", sign, s, j), zout.at[sign, s, j], zin.at[sign, s, j], at_z(step), "zr")

    zr_step(0)

    def eye_at(second):
        return (iota((GQ, SLOTS), 1) == iota((GQ, SLOTS), 0) + GQ * second).astype(F32)

    def partial_totals(i):
        row = jnp.zeros((1, SLOTS), F32)
        for second in range(2):
            a = i + second * (NZ // 2)
            column = jnp.sum(hits[a] * sum2[pl.ds(a, 1), :], axis=1, keepdims=True)
            row = row + to_row(column, eye_at(second))
        t_out[pl.ds(i, 1), :] = row

    by_groups(partial_totals, 0, NZ // 2)
    own_row, own_eye = pl.ds(z % (NZ // 2), 1), eye_at(z // (NZ // 2))
    t_out[own_row, :] = t_out[own_row, :] + to_row(weight_sum, own_eye)
    t_in[pl.ds(z, 1)] = t_out[...][None]
    for s in range(1, NZ):
        send("t", t_out, t_in.at[z], at_z(s))
    zr_step(1)

    def partial_radials(a):
        column = jnp.sum(hits[a] * sum2[pl.ds(NZ + a, 1), :], axis=1, keepdims=True)
        r_out[pl.ds(a, 1)] = to_row(column, eye(GQ, SLOTS))[None]

    by_groups(partial_radials)
    r_in[pl.ds(z, 1)] = r_out[pl.ds(z, 1)]
    for s in range(1, NZ):
        send("r", r_out.at[(z + s) % NZ], r_in.at[z], at_z(s))
    zr_step(2)

    receive("t", t_in.at[pl.ds(0, NZ - 1)])
    totals = t_in[0]
    for i in range(1, NZ):
        totals = totals + t_in[i]
    inv[...] = 1.0 / totals

    def passage_terms(a):
        hit, q_rows, p_rows = hits[a], qall[a], prow[a]
        column = to_column(inv[pl.ds(a % (NZ // 2), 1), :], eye_at(a // (NZ // 2)))
        spread = hit * column
        top = spread * k_c[pl.ds(a, 1), :]
        share_of = jnp.sum(spread, axis=0, keepdims=True) * r_c[pl.ds(a, 1), :]
        bottom = eye(SLOTS, SLOTS) * (-share_of)
        lhs = jnp.concatenate([top, bottom], axis=0).astype(BF16)
        terms = tn(lhs, jnp.concatenate([q_rows, p_rows], axis=0)).astype(BF16)
        for o in range(NX):
            cq[o, a] = terms[o * CAP : (o + 1) * CAP]

    by_groups(passage_terms, 0, NZ // 2)
    zr_step(3)
    by_groups(passage_terms, NZ // 2, NZ // 2)
    zr_step(4)

    def passage_sums(step):
        o = (x + step + NX) % NX
        gp[o] = tn(one_hot[o].reshape(NZ * CAP, GP), cq[o].reshape(NZ * CAP, COLS))

    def xr_rows(h, half):
        return slice(h * HALF + half * (HALF // 2), h * HALF + (half + 1) * (HALF // 2))

    def xr_start(h):
        for sign in range(2):
            xout[h, 0, sign] = gp[(x + 2) % NX, xr_rows(h, sign)].astype(BF16)
            send(("xr", h, sign, "far"), xout.at[h, 0, sign], xhalf.at[h, sign], at_x(1 - 2 * sign))

    def xr_own(h):
        for sign in range(2):
            near = (x + 1 - 2 * sign + NX) % NX
            xout[h, 1 + sign, 1 - sign] = gp[near, xr_rows(h, 1 - sign)].astype(BF16)
            there = xfull.at[h, sign, 1 - sign]
            send(("xr", h), xout.at[h, 1 + sign, 1 - sign], there, at_x(1 - 2 * sign))

    def xr_forward(h):
        for sign in range(2):
            near = (x + 1 - 2 * sign + NX) % NX
            receive(("xr", h, sign, "far"), xhalf.at[h, sign])
            merged = gp[near, xr_rows(h, sign)] + xhalf[h, sign].astype(F32)
            xout[h, 1 + sign, sign] = merged.astype(BF16)
            there = xfull.at[h, sign, sign]
            send(("xr", h), xout.at[h, 1 + sign, sign], there, at_x(1 - 2 * sign))

    def xr_finish(h):
        receive(("xr", h), xfull.at[h])
        value = gp[x, h * HALF : (h + 1) * HALF]
        full = xfull[h].reshape(2, HALF, COLS)
        return value + full[0].astype(F32) + full[1].astype(F32)

    class Scatter:
        def __init__(self, name, rows, part, core, out, half, full):
            self.name, self.rows = name, rows
            self.part, self.core, self.out, self.half, self.full = part, core, out, half, full
            self.places = [(y + step) % NY for step in (2, 1, 3, 0)]

        def product(self, down):
            def one(i, carry):
                columns = pl.ds(pl.multiple_of(i * 512, 512), 512)
                block = nt(down, wv[columns, :]).reshape(NY, NC, self.rows, 512)
                for k in range(NC):
                    self.part[k, :, :, columns] = block[:, k].astype(BF16)
                return carry

            lax.fori_loop(0, D // 512, one, 0)
            for i, place in enumerate(self.places):
                there = self.core.at[place]
                send((self.name, "c", i), self.part.at[1 - c, place], there, at_y(0, True))

        def arrive(self, i):
            receive((self.name, "c", i), self.core.at[self.places[i]])

        def both(self, i, h):
            place = self.places[i]
            cut = slice(h * (D // 2), (h + 1) * (D // 2))
            return self.part[c, place, :, cut].astype(F32) + self.core[place, :, cut].astype(F32)

        def start(self):
            self.arrive(0)
            for sign in range(2):
                self.out[0, sign] = self.both(0, sign).astype(BF16)
                there = self.half.at[sign]
                send((self.name, "far", sign), self.out.at[0, sign], there, at_y(1 - 2 * sign))
            for sign in range(2):
                self.arrive(1 + sign)
                self.out[1 + sign, 1 - sign] = self.both(1 + sign, 1 - sign).astype(BF16)
                there = self.full.at[sign, 1 - sign]
                send((self.name, "full"), self.out.at[1 + sign, 1 - sign], there, at_y(1 - 2 * sign))

        def forward(self):
            for sign in range(2):
                merged = self.both(1 + sign, sign)
                receive((self.name, "far", sign), self.half.at[sign])
                self.out[1 + sign, sign] = (merged + self.half[sign].astype(F32)).astype(BF16)
                there = self.full.at[sign, sign]
                send((self.name, "full"), self.out.at[1 + sign, sign], there, at_y(1 - 2 * sign))

        def finish(self, out):
            self.arrive(3)
            own = [self.both(3, h) for h in range(2)]
            receive((self.name, "full"), self.full)
            for h in range(2):
                total = own[h] + self.full[0, h].astype(F32) + self.full[1, h].astype(F32)
                out[:, h * (D // 2) : (h + 1) * (D // 2)] = total.astype(BF16)

    class NearScatter(Scatter):
        def start(self):
            for i, step in enumerate((2, 1, 3)):
                self.arrive(i)
                for h in range(2):
                    self.out[i, h] = self.both(i, h).astype(BF16)
                send((self.name, "near"), self.out.at[i], self.full.at[i], at_y(step))

        def finish(self, out):
            self.arrive(3)
            own = [self.both(3, h) for h in range(2)]
            receive((self.name, "near"), self.full)
            for h in range(2):
                total = own[h] + self.full[0, h].astype(F32)
                total = total + self.full[1, h].astype(F32) + self.full[2, h].astype(F32)
                out[:, h * (D // 2) : (h + 1) * (D // 2)] = total.astype(BF16)

    q_scatter = NearScatter("Q", QR, qpart, qcore, qout, None, qfull)
    p_scatter = [
        Scatter("P%d" % h, PC, ppart.at[h], pcore.at[h], pout.at[h], phalf.at[h], pfull.at[h])
        for h in range(2)
    ]

    passage_sums(2)
    xr_start(0)
    xr_start(1)
    passage_sums(1)
    passage_sums(-1)
    xr_own(0)
    xr_own(1)
    zr_step(5)
    passage_sums(0)

    total = 1.0 / to_column(inv[own_row, :], own_eye)
    inverse = 1.0 / total
    loss = jnp.log(total) + (1.0 - jnp.sum(positive * cosine, axis=1, keepdims=True)) / TEMPERATURE
    mine = (iota((GQ, SLOTS), 0) == g * QR + iota((GQ, SLOTS), 1)).astype(F32)
    loss_out[...] = jnp.sum(mine * loss, axis=0, keepdims=True)
    slope = (weight * inverse - positive) / TEMPERATURE
    pull = slope * cosine
    radial_p = jnp.sum(pull, axis=0, keepdims=True) / (square_p + EPSILON)
    coefficient = (slope / norm).astype(BF16)
    group_p = tn(coefficient, own_q)
    xr_forward(0)
    zr_step(6)
    down_p = []
    eye_p = eye(HALF, HALF)
    for h in range(2):
        column = to_column(radial_p[:, h * HALF : (h + 1) * HALF], eye_p)
        rows = slice(h * HALF, (h + 1) * HALF)
        down_p.append(group_p[rows] - column * own_p[rows].astype(F32))
    xr_forward(1)
    receive("r", r_in.at[pl.ds(0, NZ - 1)])
    radials = r_in[0]
    for i in range(1, NZ):
        radials = radials + r_in[i]
    radial_slots = to_column(radials, eye_q) * inverse / TEMPERATURE
    radial_q = jnp.sum(pull, axis=1, keepdims=True) + radial_slots
    group_q = nn(coefficient, own_p) - (radial_q / (square_q + EPSILON)) * own_q32
    own_terms = query_terms(z)
    zr_step(7)
    p_scatter[0].product((xr_finish(0) + down_p[0]).astype(BF16))

    p_scatter[1].product((xr_finish(1) + down_p[1]).astype(BF16))

    for sign in range(2):
        for j in range(SUBS):
            receive(("zr", sign, last, j), zin.at[sign, last, j])
    departures["zr"] = qall.at[pl.ds(0, NZ - 1)]
    from_z = own_terms + jnp.concatenate(
        [zin[0, last, j].astype(F32) + zin[1, last, j].astype(F32) for j in range(SUBS)], axis=0
    )
    factor = inverse / jnp.sqrt(square_q + EPSILON) / TEMPERATURE
    q_scatter.product((group_q + from_z * factor).astype(BF16))
    p_scatter[0].start()
    p_scatter[1].start()
    q_scatter.start()
    p_scatter[0].forward()
    p_scatter[1].forward()
    p_scatter[0].finish(pg_out.at[0:PC])
    p_scatter[1].finish(pg_out.at[PC:PR])
    q_scatter.finish(qg_out)
    depart()
    assert not departures
    assert len(names) <= CHANNELS


def place_outputs(loss, query_grad, passage_grad, loss_out, query_out, passage_out):
    loss_out[...] = loss[0, :QR]
    query_out[...] = query_grad[...]
    passage_out[...] = passage_grad[...]


def per_device(query_hidden, passage_hidden, projection, negative_ids):
    vmem = pl.BlockSpec(memory_space=pltpu.VMEM)
    hbm = pl.BlockSpec(memory_space=pl.ANY)
    v = pltpu.VMEM
    loss, query_grad, passage_grad = pl.pallas_call(
        kernel,
        out_shape=(
            jax.ShapeDtypeStruct((1, SLOTS), F32),
            jax.ShapeDtypeStruct((QR, D), BF16),
            jax.ShapeDtypeStruct((PR, D), BF16),
        ),
        in_specs=[vmem, vmem, hbm, hbm],
        out_specs=(vmem, vmem, vmem),
        scratch_shapes=[
            v((D, COLS), BF16),
            v((NEG, NZ * NX * GQ), I32),
            v((NG, QR, D), BF16),
            v((2, NG, PC, D), BF16),
            v((NZ, GQ, COLS), BF16),
            v((NX, GP, COLS), BF16),
            v((NZ, GQ, NEG), I32),
            v((NZ, GQ, SLOTS), F32),
            v((NX, NZ, CAP, GP), BF16),
            v((NZ, SLOTS, COLS), BF16),
            v((2 * GQ, SLOTS), F32),
            v((NG, 2 * GQ, SLOTS), F32),
            v((8, SLOTS), F32),
            v((NG, 8, SLOTS), F32),
            v((1, SLOTS), F32),
            v((NZ, 1, SLOTS), F32),
            v((1, GP), F32),
            v((NX, 1, GP), F32),
            v((NZ, SLOTS), F32),
            v((NZ, SLOTS), F32),
            v((NZ, SLOTS), F32),
            v((NG, NZ, SLOTS), F32),
            v((2 * NZ, SLOTS), F32),
            v((NZ, SLOTS), F32),
            v((NZ, SLOTS), F32),
            v((NZ, SLOTS), F32),
            v((NZ, SLOTS), F32),
            v((NZ // 2, SLOTS), F32),
            v((NZ, NZ // 2, SLOTS), F32),
            v((NZ // 2, SLOTS), F32),
            v((NZ, 1, SLOTS), F32),
            v((NZ, 1, SLOTS), F32),
            v((2, NZ // 2, SUBS, SUB, COLS), BF16),
            v((2, NZ // 2, SUBS, SUB, COLS), BF16),
            v((NX, NZ, CAP, COLS), BF16),
            v((NX, GP, COLS), F32),
            v((2, 3, 2, HALF // 2, COLS), BF16),
            v((2, 2, HALF // 2, COLS), BF16),
            v((2, 2, 2, HALF // 2, COLS), BF16),
            v((NC, NY, QR, D), BF16),
            v((NY, QR, D), BF16),
            v((3, 2, QR, D // 2), BF16),
            v((3, 2, QR, D // 2), BF16),
            v((2, NC, NY, PC, D), BF16),
            v((2, NY, PC, D), BF16),
            v((2, 3, 2, PC, D // 2), BF16),
            v((2, 2, PC, D // 2), BF16),
            v((2, 2, 2, PC, D // 2), BF16),
            pltpu.SemaphoreType.DMA((10,)),
            pltpu.SemaphoreType.DMA((CHANNELS,)),
            pltpu.SemaphoreType.DMA((CHANNELS,)),
        ],
        compiler_params=pltpu.CompilerParams(
            collective_id=0, has_side_effects=True, vmem_limit_bytes=56 * 1024 * 1024
        ),
    )(query_hidden, passage_hidden, projection, negative_ids.T)
    return pl.pallas_call(
        place_outputs,
        out_shape=(
            jax.ShapeDtypeStruct((QR,), F32),
            jax.ShapeDtypeStruct((QR, D), BF16),
            jax.ShapeDtypeStruct((PR, D), BF16),
        ),
        in_specs=[vmem, vmem, vmem],
        out_specs=(vmem, vmem, vmem),
    )(loss, query_grad, passage_grad)


def solution(mesh):
    in_specs = (P(("dp", "group"), None), P(("dp", "group"), None), P(None, "group"), P())
    out_specs = (P(("dp", "group")), P(("dp", "group"), None), P(("dp", "group"), None))
    return jax.shard_map(
        per_device, mesh=mesh, in_specs=in_specs, out_specs=out_specs, check_vma=False
    )
```

```python
import jax
import jax.numpy as jnp
from jax import lax
from jax.experimental import pallas as pl
from jax.experimental.pallas import tpu as pltpu
from jax.sharding import PartitionSpec as P

TEMPERATURE = 0.05
EPSILON = 1e-06
MESH = pl.DeviceIdType.MESH
F32, BF16, I32 = jnp.float32, jnp.bfloat16, jnp.int32

NZ, NX, NY, NC = 16, 4, 4, 2
NG = NY * NC
D = 4096
COLS = D // NG
QR, PR, PC = 8, 32, 16
GQ, GP = QR * NG, PR * NG
HALF = GP // 2
NEG, CAP = 16, 32
SLOTS = NX * CAP
CHANNELS = 256
SUBS = 2
SUB = GQ // SUBS


def nn(a, b):
    return lax.dot_general(a, b, (((1,), (0,)), ((), ())), preferred_element_type=F32)


def nt(a, b):
    return lax.dot_general(a, b, (((1,), (1,)), ((), ())), preferred_element_type=F32)


def tn(a, b):
    return lax.dot_general(a, b, (((0,), (0,)), ((), ())), preferred_element_type=F32)


def iota(shape, dim):
    return lax.broadcasted_iota(I32, shape, dim)


def eye(rows, columns):
    return (iota((rows, columns), 0) == iota((rows, columns), 1)).astype(F32)


def to_row(column, identity):
    return jnp.sum(identity * column, axis=0, keepdims=True)


def to_column(row, identity):
    return jnp.sum(identity * row, axis=1, keepdims=True)


def kernel(
    qh, ph, weight_hbm, ids_hbm,
    loss_out, qg_out, pg_out,
    wv, idv, hq, hp, qall, pall, code, hits, one_hot, prow,
    pay1, got1, payn, gotn, nz_out, nz_in, nx_out, nx_in, sl_q, sl_p,
    pay2, got2, sum2, fill, w_p, k_c, r_c, t_out, t_in, inv, r_out, r_in,
    zout, zin, turned_k, turned_hot, cq, gp, xout, xhalf, xfull,
    qpart, qcore, qout, qfull, ppart, pcore, pout, phalf, pfull,
    local_sem, send_sem, recv_sem,
):
    dp, g = lax.axis_index("dp"), lax.axis_index("group")
    z, x = dp // NX, dp % NX
    y, c = g // NC, g % NC

    def at_z(step):
        return (((z + step + 2 * NZ) % NZ) * NX + x, g)

    def at_x(step):
        return (z * NX + (x + step + NX) % NX, g)

    def member(step, other):
        return ((y + step + NY) % NY) * NC + (1 - c if other else c)

    def at_y(step, other=False):
        return (dp, member(step, other))

    others = [(s, o) for s in (0, 1, 2, 3) for o in (False, True) if (s, o) != (0, False)]

    names, departures = {}, {}

    def channel(name):
        return names.setdefault(name, len(names))

    def copy(name, group, src, dst, device):
        return pltpu.make_async_remote_copy(
            src_ref=src, dst_ref=dst, send_sem=send_sem.at[channel(("from", group))],
            recv_sem=recv_sem.at[channel(name)], device_id=device, device_id_type=MESH,
        )

    def send(name, src, dst, device, group=None):
        group = name if group is None else group
        departures.setdefault(group, None)
        copy(name, group, src, dst, device).start()

    def receive(name, dst):
        if name in departures:
            departures[name] = dst
        copy(name, name, dst, dst, at_x(1)).wait_recv()

    def depart():
        for group, ref in list(departures.items()):
            if ref is not None:
                copy(group, group, ref, ref, at_x(1)).wait_send()
                del departures[group]

    w_copies = []
    for k in range(8):
        rows = pl.ds(k * COLS, COLS)
        w_copies.append(pltpu.make_async_copy(weight_hbm.at[rows], wv.at[rows], local_sem.at[2 + k]))
        w_copies[-1].start()
    id_copy = pltpu.make_async_copy(ids_hbm, idv, local_sem.at[1])
    id_copy.start()
    barrier = pltpu.get_barrier_semaphore()
    greeted = [at_z(s) for s in range(1, NZ)] + [at_x(s) for s in range(1, NX)] + [at_y(*o) for o in others]
    for device in greeted:
        pl.semaphore_signal(barrier, inc=1, device_id=device, device_id_type=MESH)
    pl.semaphore_wait(barrier, len(greeted))

    def columns(h):
        return pl.ds(h * (D // 2), D // 2)

    class Gather:
        def __init__(self, name, src, held):
            self.name, self.src, self.held = name, src, held

        def start(self):
            for k in range(2):
                for sign, step in ((0, 1), (1, -1)):
                    h = k if sign == 0 else 1 - k
                    here = self.held.at[g, :, columns(h)]
                    send((self.name, sign, h), self.src.at[:, columns(h)], here, at_y(step))
            send((self.name, "c"), self.src, self.held.at[g], at_y(0, True))
            self.held[pl.ds(g, 1)] = self.src[...][None]

        def forward(self):
            for k in range(2):
                for sign, step in ((0, 1), (1, -1)):
                    h = k if sign == 0 else 1 - k
                    block = member(-step, False)
                    piece = self.held.at[block, :, columns(h)]
                    receive((self.name, sign, h), piece)
                    if k == 0:
                        send((self.name, "far"), piece, piece, at_y(step))
                    else:
                        whole = self.held.at[block]
                        send((self.name, "c"), whole, whole, at_y(0, True))

        def forward_far(self):
            whole = self.held.at[member(2, False)]
            receive((self.name, "far"), whole)
            send((self.name, "c"), whole, whole, at_y(0, True))

        def finish(self):
            receive((self.name, "c"), self.held.at[pl.ds(0, NY)])

    class Near:
        def __init__(self, name, src, held):
            self.name, self.src, self.held = name, src, held

        def start(self):
            for step in (2, 1, 3):
                send((self.name, step), self.src, self.held.at[g], at_y(step))
            send((self.name, "c"), self.src, self.held.at[g], at_y(0, True))
            self.held[pl.ds(g, 1)] = self.src[...][None]

        def forward(self):
            for step in (1, 3, 2):
                block = self.held.at[member(-step, False)]
                receive((self.name, step), block)
                send((self.name, "c"), block, block, at_y(0, True))

        def finish(self):
            receive((self.name, "c"), self.held.at[pl.ds(0, NY)])

    q_gather = Near("q", qh, hq)
    p_gather = [Gather("p%d" % h, ph.at[pl.ds(h * PC, PC)], hp.at[h]) for h in range(2)]

    last = NZ // 2 - 1

    def halved(sign):
        return range(sign * SUBS // 2, (sign + 1) * SUBS // 2)

    def z_piece(sign, s, j):
        block = (z - (1 - 2 * sign) * s + 2 * NZ) % NZ
        return qall.at[block, pl.ds(j * SUB, SUB)]

    def z_step(s):
        for j in range(SUBS):
            for sign in range(2):
                if s < last or j in halved(sign):
                    piece = z_piece(sign, s, j)
                    if s > 0:
                        receive(("z", sign, s - 1, j), piece)
                    send(("z", sign, s, j), piece, piece, at_z(1 - 2 * sign), "z")

    def z_finish():
        for j in range(SUBS):
            for sign in range(2):
                s = last if j in halved(sign) else last - 1
                receive(("z", sign, s, j), z_piece(sign, s + 1, j))
        departures["z"] = qall.at[pl.ds(0, NZ - 1)]

    def x_piece(block, h, half):
        return pall.at[block, pl.ds(h * HALF + half * (HALF // 2), HALF // 2)]

    def x_start(h):
        for k in range(2):
            for sign in range(2):
                half = k if sign == 0 else 1 - k
                piece = x_piece(x, h, half)
                send(("x", h, sign, half), piece, piece, at_x(1 - 2 * sign))

    def x_forward(h):
        for sign in range(2):
            step = 1 - 2 * sign
            piece = x_piece((x - step + NX) % NX, h, sign)
            receive(("x", h, sign, sign), piece)
            send(("x", h, "far"), piece, piece, at_x(step))

    def x_finish(h):
        for sign in range(2):
            step = 1 - 2 * sign
            receive(("x", h, sign, 1 - sign), x_piece((x - step + NX) % NX, h, 1 - sign))
        receive(("x", h, "far"), pall.at[(x + 2) % NX, pl.ds(h * HALF, HALF)])

    def find_slots():
        pieces = []
        for a in range(NZ):
            start = pl.multiple_of(a * NX * GQ + (x // 2) * 2 * GQ, 2 * GQ)
            pieces.append(idv[:, pl.ds(start, 2 * GQ)].astype(F32))
        turned = jnp.concatenate(pieces, axis=0).T
        odd = (x % 2).astype(F32)
        ids = (turned[:GQ] * (1.0 - odd) + turned[GQ:] * odd).astype(I32)
        owner = (ids >> 8) - z * NX
        place = ids & 255
        place = ((place >> 4) & 1) * HALF + (place >> 5) * PC + (place & 15)
        mine = jnp.concatenate([(owner == o).astype(F32) for o in range(NX)], axis=0)
        picked = mine.astype(BF16)
        shape = (NX * GQ, NZ * NEG)
        i, j = iota(shape, 0), iota(shape, 1)
        before = ((i // GQ == j // GQ) & (j < i)).astype(F32).astype(BF16)
        same = i // NEG == j // NEG
        ahead = (same & (i < j)).astype(F32).astype(BF16)
        row_sums = nn(before, picked).astype(BF16)
        rank = nn(row_sums, same.astype(F32).astype(BF16)) + nn(picked, ahead)
        slot = mine * (rank + ((i // GQ) * CAP + 1).astype(F32))
        slot = slot[:GQ] + slot[GQ : 2 * GQ] + slot[2 * GQ : 3 * GQ] + slot[3 * GQ :]
        both = slot.astype(I32) * 256 + place
        both = jnp.where(slot > 0.0, both, 0)
        for a in range(NZ):
            code[a] = both[:, a * NEG : (a + 1) * NEG]

    def fill_slots(first, count):
        def one(a, carry):
            block = code[a]
            lane = iota((GQ, SLOTS), 1) + 1
            hit = jnp.zeros((GQ, SLOTS), F32)
            spot = jnp.zeros((GQ, SLOTS), I32)
            for k in range(NEG):
                column = jnp.broadcast_to(block[:, k : k + 1], (GQ, SLOTS))
                found = (column >> 8) == lane
                hit = jnp.where(found, 1.0, hit)
                spot = jnp.where(found, column & 255, spot)
            hits[a] = hit
            fill[pl.ds(a, 1), :] = jnp.sum(hit, axis=0, keepdims=True)
            row = jnp.sum(spot.astype(F32), axis=0, keepdims=True)
            column = to_column(row, eye(SLOTS, SLOTS)).astype(I32)
            chosen = (iota((SLOTS, GP), 1) == column).astype(F32).astype(BF16)
            for o in range(NX):
                one_hot[o, a] = chosen[o * CAP : (o + 1) * CAP]
            return carry

        lax.fori_loop(first, first + count, one, 0)

    def share(name, pay, got):
        for step, other in others:
            send(name, pay, got.at[g], at_y(step, other))

    def collect(name, pay, got):
        got[pl.ds(g, 1)] = pay[...][None]
        receive(name, got.at[pl.ds(0, NG - 1)])
        total = got[0]
        for i in range(1, NG):
            total = total + got[i]
        return total

    def project_passages(h):
        rows = hp[h].reshape(HALF, D)
        pall[pl.ds(x, 1), h * HALF : (h + 1) * HALF] = nn(rows, wv[...]).astype(BF16)[None]
        x_start(h)

    eye_q, eye_s = eye(GQ, SLOTS), eye(SLOTS, SLOTS)
    p_first, p_second = p_gather

    q_gather.start()
    p_first.start()
    id_copy.wait()
    find_slots()
    q_gather.forward()
    p_second.start()
    fill_slots(0, 6)
    q_gather.finish()
    rows = hq[...].astype(F32).reshape(GQ, D).astype(BF16)
    projected = jnp.zeros((GQ, COLS), F32)
    for k, one in enumerate(w_copies):
        one.wait()
        part = slice(k * COLS, (k + 1) * COLS)
        projected = projected + nn(rows[:, part], wv[part, :])
    qall[pl.ds(z, 1)] = projected.astype(BF16)[None]
    z_step(0)
    p_first.forward()
    fill_slots(6, 2)
    p_second.forward()
    z_step(1)
    p_first.forward_far()
    fill_slots(8, 2)
    p_first.finish()
    z_step(2)
    project_passages(0)
    p_second.forward_far()
    z_step(3)
    p_second.finish()
    project_passages(1)
    z_step(4)

    own_q, own_p = qall[z], pall[x]
    for h in range(2):
        part = own_p[h * HALF : (h + 1) * HALF]
        payn[h : h + 1] = jnp.sum(nt(part, part) * eye_s, axis=0, keepdims=True)
    own_q32 = own_q.astype(F32)
    payn[2:3] = to_row(jnp.sum(own_q32 * own_q32, axis=1, keepdims=True), eye_q)
    payn[3:] = jnp.zeros((payn.shape[0] - 3, SLOTS), F32)
    share("n", payn, gotn)

    inner = nt(own_q, own_p)
    pay1[0:GQ] = inner[:, :SLOTS]
    pay1[GQ:] = inner[:, SLOTS:]
    share("s1", pay1, got1)
    x_forward(0)
    z_step(5)
    fill_slots(10, 4)
    sums = collect("n", payn, gotn)
    square_p = jnp.concatenate([sums[0:1], sums[1:2]], axis=1)
    square_q = to_column(sums[2:3], eye_q)
    nz_out[...] = sums[2:3]
    nx_out[...] = square_p
    nz_in[pl.ds(z, 1)] = sums[2:3][None]
    nx_in[pl.ds(x, 1)] = square_p[None]
    for s in range(1, NX):
        send("nx", nx_out, nx_in.at[x], at_x(s))
    for s in range(1, NZ):
        send("nz", nz_out, nz_in.at[z], at_z(s))
    x_forward(1)
    z_step(6)
    fill_slots(14, 2)
    x_finish(0)
    z_step(7)
    x_finish(1)

    for o in range(NX):
        chosen = nn(one_hot[o].reshape(NZ * CAP, GP), pall[o])
        prow[:, o * CAP : (o + 1) * CAP, :] = chosen.astype(BF16).reshape(NZ, CAP, COLS)

    def by_groups(one, first=0, count=NZ, width=4):
        def some(i, carry):
            for k in range(width):
                one(first + i * width + k)
            return carry

        lax.fori_loop(0, count // width, some, 0)

    def pair_products(step):
        a = (z + step + 2 * NZ) % NZ
        products = nt(qall[a], prow[a])
        pay2[pl.ds(a, 1), :] = jnp.sum(products * hits[a], axis=0, keepdims=True)

    by_groups(pair_products, 2 - NZ // 2, NZ - 4)
    z_finish()
    for step in (NZ // 2 - 2, NZ // 2 - 1, NZ // 2, NZ // 2 + 1):
        pair_products(step)
    share("s2", pay2, got2)

    receive("nx", nx_in.at[pl.ds(0, NX - 1)])
    receive("nz", nz_in.at[pl.ds(0, NZ - 1)])

    depart()

    def slot_norms(a):
        column = to_column(nz_in[a], eye(GQ, SLOTS))
        sl_q[pl.ds(a, 1), :] = jnp.sum(hits[a] * column, axis=0, keepdims=True)
        columns = [
            jnp.sum(one_hot[o, a].astype(F32) * nx_in[o], axis=1, keepdims=True) for o in range(NX)
        ]
        sl_p[pl.ds(a, 1), :] = to_row(jnp.concatenate(columns, axis=0), eye(SLOTS, SLOTS))

    by_groups(slot_norms)

    sums = collect("s1", pay1, got1)
    inner = jnp.concatenate([sums[0:GQ], sums[GQ : 2 * GQ]], axis=1)
    norm = jnp.sqrt(square_q + EPSILON) * jnp.sqrt(square_p + EPSILON)
    cosine = inner / norm
    weight = jnp.exp((cosine - 1.0) / TEMPERATURE)
    weight_sum = jnp.sum(weight, axis=1, keepdims=True)
    spot = iota((GQ, GP), 1)
    passage = ((spot >> 4) & 7) * PR + (spot >> 7) * PC + (spot & 15)
    positive = (passage == iota((GQ, GP), 0) * 4).astype(F32)

    inner_slot = collect("s2", pay2, got2)
    square_slot_p = sl_p[...]
    norm_slot_q = jnp.sqrt(sl_q[...] + EPSILON)
    norm_slot_p = jnp.sqrt(square_slot_p + EPSILON)
    cosine_slot = inner_slot / (norm_slot_q * norm_slot_p)
    weight_slot = jnp.exp((cosine_slot - 1.0) / TEMPERATURE) * fill[...]
    sum2[0:NZ] = weight_slot
    sum2[NZ:] = weight_slot * cosine_slot
    w_p[...] = weight_slot / norm_slot_p
    k_c[...] = weight_slot / (norm_slot_q * norm_slot_p) / TEMPERATURE
    r_c[...] = weight_slot * cosine_slot / (square_slot_p + EPSILON) / TEMPERATURE

    def query_terms(a):
        coefficient = (hits[a] * w_p[pl.ds(a, 1), :]).astype(BF16)
        return nn(coefficient, prow[a])

    def zr_step(s):
        far = query_terms((z + NZ // 2) % NZ) if s == 0 else None
        terms = []
        for sign, step in ((0, 1), (1, -1)):
            block = (z + step * (NZ // 2 - s) + NZ) % NZ
            terms.append(far if s == 0 else query_terms(block))
        for j in range(SUBS):
            for sign, step in ((0, 1), (1, -1)):
                if s == 0 and j not in halved(sign):
                    continue
                value = terms[sign][j * SUB : (j + 1) * SUB]
                if s > 1 or (s == 1 and j in halved(sign)):
                    receive(("zr", sign, s - 1, j), zin.at[sign, s - 1, j])
                    value = value + zin[sign, s - 1, j].astype(F32)
                zout[sign, s, j] = value.astype(BF16)
                send(("zr", sign, s, j), zout.at[sign, s, j], zin.at[sign, s, j], at_z(step), "zr")

    def eye_at(second):
        return (iota((GQ, SLOTS), 1) == iota((GQ, SLOTS), 0) + GQ * second).astype(F32)

    def partial_totals(i):
        row = jnp.zeros((1, SLOTS), F32)
        for second in range(2):
            a = i + second * (NZ // 2)
            column = jnp.sum(hits[a] * sum2[pl.ds(a, 1), :], axis=1, keepdims=True)
            row = row + to_row(column, eye_at(second))
        t_out[pl.ds(i, 1), :] = row

    by_groups(partial_totals, 0, NZ // 2)
    own_row, own_eye = pl.ds(z % (NZ // 2), 1), eye_at(z // (NZ // 2))
    t_out[own_row, :] = t_out[own_row, :] + to_row(weight_sum, own_eye)
    t_in[pl.ds(z, 1)] = t_out[...][None]
    for s in range(1, NZ):
        send("t", t_out, t_in.at[z], at_z(s))
    zr_step(0)

    def turn_terms(a):
        turned_k[a] = (hits[a] * k_c[pl.ds(a, 1), :]).T.astype(BF16)

    by_groups(turn_terms)
    zr_step(1)
    for o in range(NX):
        turned_hot[o] = one_hot[o].reshape(NZ * CAP, GP).astype(F32).T.astype(BF16)

    receive("t", t_in.at[pl.ds(0, NZ - 1)])
    totals = t_in[0]
    for i in range(1, NZ):
        totals = totals + t_in[i]
    inv[...] = 1.0 / totals

    def passage_terms(a):
        column = to_column(inv[pl.ds(a % (NZ // 2), 1), :], eye_at(a // (NZ // 2)))
        scaled = (qall[a].astype(F32) * column).astype(BF16)
        shares = jnp.sum(hits[a] * column, axis=0, keepdims=True) * r_c[pl.ds(a, 1), :]
        pulls = (eye(SLOTS, SLOTS) * (-shares)).astype(BF16)
        lhs = jnp.concatenate([pulls, turned_k[a]], axis=1)
        terms = nn(lhs, jnp.concatenate([prow[a], scaled], axis=0)).astype(BF16)
        for o in range(NX):
            cq[o, a] = terms[o * CAP : (o + 1) * CAP]

    by_groups(passage_terms, 0, NZ // 2)
    zr_step(2)
    by_groups(passage_terms, NZ // 2, NZ // 2)
    zr_step(3)

    def passage_sums(step):
        o = (x + step + NX) % NX
        gp[o] = nn(turned_hot[o], cq[o].reshape(NZ * CAP, COLS))

    def xr_rows(h, half):
        return slice(h * HALF + half * (HALF // 2), h * HALF + (half + 1) * (HALF // 2))

    def xr_start(h):
        for sign in range(2):
            xout[h, 0, sign] = gp[(x + 2) % NX, xr_rows(h, sign)].astype(BF16)
            send(("xr", h, sign, "far"), xout.at[h, 0, sign], xhalf.at[h, sign], at_x(1 - 2 * sign))

    def xr_own(h):
        for sign in range(2):
            near = (x + 1 - 2 * sign + NX) % NX
            xout[h, 1 + sign, 1 - sign] = gp[near, xr_rows(h, 1 - sign)].astype(BF16)
            there = xfull.at[h, sign, 1 - sign]
            send(("xr", h), xout.at[h, 1 + sign, 1 - sign], there, at_x(1 - 2 * sign))

    def xr_forward(h):
        for sign in range(2):
            near = (x + 1 - 2 * sign + NX) % NX
            receive(("xr", h, sign, "far"), xhalf.at[h, sign])
            merged = gp[near, xr_rows(h, sign)] + xhalf[h, sign].astype(F32)
            xout[h, 1 + sign, sign] = merged.astype(BF16)
            there = xfull.at[h, sign, sign]
            send(("xr", h), xout.at[h, 1 + sign, sign], there, at_x(1 - 2 * sign))

    def xr_finish(h):
        receive(("xr", h), xfull.at[h])
        value = gp[x, h * HALF : (h + 1) * HALF]
        full = xfull[h].reshape(2, HALF, COLS)
        return value + full[0].astype(F32) + full[1].astype(F32)

    class Scatter:
        def __init__(self, name, rows, part, core, out, half, full):
            self.name, self.rows = name, rows
            self.part, self.core, self.out, self.half, self.full = part, core, out, half, full
            self.places = [(y + step) % NY for step in (2, 1, 3, 0)]

        def part_out(self, block, columns):
            block = block.reshape(NY, NC, self.rows, 512)
            for k in range(NC):
                self.part[k, :, :, columns] = block[:, k].astype(BF16)

        def to_core(self):
            for i, place in enumerate(self.places):
                there = self.core.at[place]
                send((self.name, "c", i), self.part.at[1 - c, place], there, at_y(0, True))

        def arrive(self, i):
            receive((self.name, "c", i), self.core.at[self.places[i]])

        def both(self, i, h):
            place = self.places[i]
            cut = slice(h * (D // 2), (h + 1) * (D // 2))
            return self.part[c, place, :, cut].astype(F32) + self.core[place, :, cut].astype(F32)

        def start(self):
            self.arrive(0)
            for sign in range(2):
                self.out[0, sign] = self.both(0, sign).astype(BF16)
                there = self.half.at[sign]
                send((self.name, "far", sign), self.out.at[0, sign], there, at_y(1 - 2 * sign))
            for sign in range(2):
                self.arrive(1 + sign)
                self.out[1 + sign, 1 - sign] = self.both(1 + sign, 1 - sign).astype(BF16)
                there = self.full.at[sign, 1 - sign]
                send((self.name, "full"), self.out.at[1 + sign, 1 - sign], there, at_y(1 - 2 * sign))

        def forward(self):
            for sign in range(2):
                merged = self.both(1 + sign, sign)
                receive((self.name, "far", sign), self.half.at[sign])
                self.out[1 + sign, sign] = (merged + self.half[sign].astype(F32)).astype(BF16)
                there = self.full.at[sign, sign]
                send((self.name, "full"), self.out.at[1 + sign, sign], there, at_y(1 - 2 * sign))

        def finish(self, out):
            self.arrive(3)
            own = [self.both(3, h) for h in range(2)]
            receive((self.name, "full"), self.full)
            for h in range(2):
                total = own[h] + self.full[0, h].astype(F32) + self.full[1, h].astype(F32)
                out[:, h * (D // 2) : (h + 1) * (D // 2)] = total.astype(BF16)

    class NearScatter(Scatter):
        def start(self):
            for i, step in enumerate((2, 1, 3)):
                self.arrive(i)
                for h in range(2):
                    self.out[i, h] = self.both(i, h).astype(BF16)
                send((self.name, "near"), self.out.at[i], self.full.at[i], at_y(step))

        def finish(self, out):
            self.arrive(3)
            own = [self.both(3, h) for h in range(2)]
            receive((self.name, "near"), self.full)
            for h in range(2):
                total = own[h] + self.full[0, h].astype(F32)
                total = total + self.full[1, h].astype(F32) + self.full[2, h].astype(F32)
                out[:, h * (D // 2) : (h + 1) * (D // 2)] = total.astype(BF16)

    def project_back(scatters, downs):
        down = jnp.concatenate(downs, axis=0)

        def one(i, carry):
            columns = pl.ds(pl.multiple_of(i * 512, 512), 512)
            block = nt(down, wv[columns, :])
            first = 0
            for scatter in scatters:
                count = NG * scatter.rows
                scatter.part_out(block[first : first + count], columns)
                first += count
            return carry

        lax.fori_loop(0, D // 512, one, 0)
        for scatter in scatters:
            scatter.to_core()

    q_scatter = NearScatter("Q", QR, qpart, qcore, qout, None, qfull)
    p_scatter = [
        Scatter("P%d" % h, PC, ppart.at[h], pcore.at[h], pout.at[h], phalf.at[h], pfull.at[h])
        for h in range(2)
    ]

    passage_sums(2)
    xr_start(0)
    xr_start(1)
    passage_sums(1)
    passage_sums(-1)
    xr_own(0)
    xr_own(1)
    zr_step(4)
    passage_sums(0)
    def partial_radials(a):
        column = jnp.sum(hits[a] * sum2[pl.ds(NZ + a, 1), :], axis=1, keepdims=True)
        r_out[pl.ds(a, 1)] = to_row(column, eye(GQ, SLOTS))[None]

    by_groups(partial_radials)
    r_in[pl.ds(z, 1)] = r_out[pl.ds(z, 1)]
    for s in range(1, NZ):
        send("r", r_out.at[(z + s) % NZ], r_in.at[z], at_z(s))


    total = 1.0 / to_column(inv[own_row, :], own_eye)
    inverse = 1.0 / total
    loss = jnp.log(total) + (1.0 - jnp.sum(positive * cosine, axis=1, keepdims=True)) / TEMPERATURE
    mine = (iota((GQ, SLOTS), 0) == g * QR + iota((GQ, SLOTS), 1)).astype(F32)
    loss_out[...] = jnp.sum(mine * loss, axis=0, keepdims=True)
    slope = (weight * inverse - positive) / TEMPERATURE
    pull = slope * cosine
    radial_p = jnp.sum(pull, axis=0, keepdims=True) / (square_p + EPSILON)
    coefficient = (slope / norm).astype(BF16)
    zr_step(5)
    group_p = tn(coefficient, own_q)
    xr_forward(0)
    xr_forward(1)
    zr_step(6)
    down_p = []
    eye_p = eye(HALF, HALF)
    for h in range(2):
        column = to_column(radial_p[:, h * HALF : (h + 1) * HALF], eye_p)
        rows = slice(h * HALF, (h + 1) * HALF)
        down_p.append(group_p[rows] - column * own_p[rows].astype(F32))
    receive("r", r_in.at[pl.ds(0, NZ - 1)])
    radials = r_in[0]
    for i in range(1, NZ):
        radials = radials + r_in[i]
    radial_slots = to_column(radials, eye_q) * inverse / TEMPERATURE
    radial_q = jnp.sum(pull, axis=1, keepdims=True) + radial_slots
    group_q = nn(coefficient, own_p) - (radial_q / (square_q + EPSILON)) * own_q32
    own_terms = query_terms(z)
    zr_step(7)
    project_back([p_scatter[0]], [(xr_finish(0) + down_p[0]).astype(BF16)])
    second_p = (xr_finish(1) + down_p[1]).astype(BF16)
    p_scatter[0].start()

    for sign in range(2):
        for j in range(SUBS):
            receive(("zr", sign, last, j), zin.at[sign, last, j])
    departures["zr"] = qall.at[pl.ds(0, NZ - 1)]
    from_z = own_terms + jnp.concatenate(
        [zin[0, last, j].astype(F32) + zin[1, last, j].astype(F32) for j in range(SUBS)], axis=0
    )
    factor = inverse / jnp.sqrt(square_q + EPSILON) / TEMPERATURE
    down_q = (group_q + from_z * factor).astype(BF16)
    project_back([p_scatter[1], q_scatter], [second_p, down_q])
    p_scatter[0].forward()
    p_scatter[1].start()
    q_scatter.start()
    p_scatter[0].finish(pg_out.at[0:PC])
    p_scatter[1].forward()
    q_scatter.finish(qg_out)
    p_scatter[1].finish(pg_out.at[PC:PR])
    depart()
    assert not departures
    assert len(names) <= CHANNELS


def place_outputs(loss, query_grad, passage_grad, loss_out, query_out, passage_out):
    loss_out[...] = loss[0, :QR]
    query_out[...] = query_grad[...]
    passage_out[...] = passage_grad[...]


def per_device(query_hidden, passage_hidden, projection, negative_ids):
    vmem = pl.BlockSpec(memory_space=pltpu.VMEM)
    hbm = pl.BlockSpec(memory_space=pl.ANY)
    v = pltpu.VMEM
    loss, query_grad, passage_grad = pl.pallas_call(
        kernel,
        out_shape=(
            jax.ShapeDtypeStruct((1, SLOTS), F32),
            jax.ShapeDtypeStruct((QR, D), BF16),
            jax.ShapeDtypeStruct((PR, D), BF16),
        ),
        in_specs=[vmem, vmem, hbm, hbm],
        out_specs=(vmem, vmem, vmem),
        scratch_shapes=[
            v((D, COLS), BF16),
            v((NEG, NZ * NX * GQ), I32),
            v((NG, QR, D), BF16),
            v((2, NG, PC, D), BF16),
            v((NZ, GQ, COLS), BF16),
            v((NX, GP, COLS), BF16),
            v((NZ, GQ, NEG), I32),
            v((NZ, GQ, SLOTS), F32),
            v((NX, NZ, CAP, GP), BF16),
            v((NZ, SLOTS, COLS), BF16),
            v((2 * GQ, SLOTS), F32),
            v((NG, 2 * GQ, SLOTS), F32),
            v((8, SLOTS), F32),
            v((NG, 8, SLOTS), F32),
            v((1, SLOTS), F32),
            v((NZ, 1, SLOTS), F32),
            v((1, GP), F32),
            v((NX, 1, GP), F32),
            v((NZ, SLOTS), F32),
            v((NZ, SLOTS), F32),
            v((NZ, SLOTS), F32),
            v((NG, NZ, SLOTS), F32),
            v((2 * NZ, SLOTS), F32),
            v((NZ, SLOTS), F32),
            v((NZ, SLOTS), F32),
            v((NZ, SLOTS), F32),
            v((NZ, SLOTS), F32),
            v((NZ // 2, SLOTS), F32),
            v((NZ, NZ // 2, SLOTS), F32),
            v((NZ // 2, SLOTS), F32),
            v((NZ, 1, SLOTS), F32),
            v((NZ, 1, SLOTS), F32),
            v((2, NZ // 2, SUBS, SUB, COLS), BF16),
            v((2, NZ // 2, SUBS, SUB, COLS), BF16),
            v((NZ, SLOTS, GQ), BF16),
            v((NX, GP, NZ * CAP), BF16),
            v((NX, NZ, CAP, COLS), BF16),
            v((NX, GP, COLS), F32),
            v((2, 3, 2, HALF // 2, COLS), BF16),
            v((2, 2, HALF // 2, COLS), BF16),
            v((2, 2, 2, HALF // 2, COLS), BF16),
            v((NC, NY, QR, D), BF16),
            v((NY, QR, D), BF16),
            v((3, 2, QR, D // 2), BF16),
            v((3, 2, QR, D // 2), BF16),
            v((2, NC, NY, PC, D), BF16),
            v((2, NY, PC, D), BF16),
            v((2, 3, 2, PC, D // 2), BF16),
            v((2, 2, PC, D // 2), BF16),
            v((2, 2, 2, PC, D // 2), BF16),
            pltpu.SemaphoreType.DMA((10,)),
            pltpu.SemaphoreType.DMA((CHANNELS,)),
            pltpu.SemaphoreType.DMA((CHANNELS,)),
        ],
        compiler_params=pltpu.CompilerParams(
            collective_id=0, has_side_effects=True, vmem_limit_bytes=56 * 1024 * 1024
        ),
    )(query_hidden, passage_hidden, projection, negative_ids.T)
    return pl.pallas_call(
        place_outputs,
        out_shape=(
            jax.ShapeDtypeStruct((QR,), F32),
            jax.ShapeDtypeStruct((QR, D), BF16),
            jax.ShapeDtypeStruct((PR, D), BF16),
        ),
        in_specs=[vmem, vmem, vmem],
        out_specs=(vmem, vmem, vmem),
    )(loss, query_grad, passage_grad)


def solution(mesh):
    in_specs = (P(("dp", "group"), None), P(("dp", "group"), None), P(None, "group"), P())
    out_specs = (P(("dp", "group")), P(("dp", "group"), None), P(("dp", "group"), None))
    return jax.shard_map(
        per_device, mesh=mesh, in_specs=in_specs, out_specs=out_specs, check_vma=False
    )
```

```python
import jax
import jax.numpy as jnp
from jax import lax
from jax.experimental import pallas as pl
from jax.experimental.pallas import tpu as pltpu
from jax.sharding import PartitionSpec as P

TEMPERATURE = 0.05
EPSILON = 1e-06
MESH = pl.DeviceIdType.MESH
F32, BF16, I32 = jnp.float32, jnp.bfloat16, jnp.int32

NZ, NX, NY, NC = 16, 4, 4, 2
NG = NY * NC
D = 4096
COLS = D // NG
QR, PR, PC = 8, 32, 16
GQ, GP = QR * NG, PR * NG
HALF = GP // 2
NEG, CAP = 16, 32
SLOTS = NX * CAP
CHANNELS = 256
SUBS = 2
SUB = GQ // SUBS


def nn(a, b):
    return lax.dot_general(a, b, (((1,), (0,)), ((), ())), preferred_element_type=F32)


def nt(a, b):
    return lax.dot_general(a, b, (((1,), (1,)), ((), ())), preferred_element_type=F32)


def tn(a, b):
    return lax.dot_general(a, b, (((0,), (0,)), ((), ())), preferred_element_type=F32)


def iota(shape, dim):
    return lax.broadcasted_iota(I32, shape, dim)


def eye(rows, columns):
    return (iota((rows, columns), 0) == iota((rows, columns), 1)).astype(F32)


def to_row(column, identity):
    return jnp.sum(identity * column, axis=0, keepdims=True)


def to_column(row, identity):
    return jnp.sum(identity * row, axis=1, keepdims=True)


def kernel(
    qh, ph, weight_hbm, ids_hbm,
    loss_out, qg_out, pg_out,
    wv, idv, hq, hp, qall, pall, code, hits, one_hot, prow,
    pay1, got1, payn, gotn, nz_out, nz_in, nx_out, nx_in, sl_q, sl_p,
    pay2, got2, sum2, fill, w_p, k_c, r_c, t_out, t_in, inv, r_out, r_in,
    zout, zin, turned_k, turned_hot, cq, gp, xout, xhalf, xfull,
    qpart, qcore, qout, qfull, ppart, pcore, pout, phalf, pfull,
    local_sem, send_sem, recv_sem,
):
    dp, g = lax.axis_index("dp"), lax.axis_index("group")
    z, x = dp // NX, dp % NX
    y, c = g // NC, g % NC

    def at_z(step):
        return (((z + step + 2 * NZ) % NZ) * NX + x, g)

    def at_x(step):
        return (z * NX + (x + step + NX) % NX, g)

    def member(step, other):
        return ((y + step + NY) % NY) * NC + (1 - c if other else c)

    def at_y(step, other=False):
        return (dp, member(step, other))

    others = [(s, o) for s in (0, 1, 2, 3) for o in (False, True) if (s, o) != (0, False)]

    names, departures = {}, {}

    def channel(name):
        return names.setdefault(name, len(names))

    def copy(name, group, src, dst, device):
        return pltpu.make_async_remote_copy(
            src_ref=src, dst_ref=dst, send_sem=send_sem.at[channel(("from", group))],
            recv_sem=recv_sem.at[channel(name)], device_id=device, device_id_type=MESH,
        )

    def send(name, src, dst, device, group=None):
        group = name if group is None else group
        departures.setdefault(group, None)
        copy(name, group, src, dst, device).start()

    def receive(name, dst):
        if name in departures:
            departures[name] = dst
        copy(name, name, dst, dst, at_x(1)).wait_recv()

    def depart():
        for group, ref in list(departures.items()):
            if ref is not None:
                copy(group, group, ref, ref, at_x(1)).wait_send()
                del departures[group]

    w_copies = []
    for k in range(8):
        rows = pl.ds(k * COLS, COLS)
        w_copies.append(pltpu.make_async_copy(weight_hbm.at[rows], wv.at[rows], local_sem.at[2 + k]))
        w_copies[-1].start()
    id_copy = pltpu.make_async_copy(ids_hbm, idv, local_sem.at[1])
    id_copy.start()
    barrier = pltpu.get_barrier_semaphore()
    greeted = [at_z(s) for s in range(1, NZ)] + [at_x(s) for s in range(1, NX)] + [at_y(*o) for o in others]
    for device in greeted:
        pl.semaphore_signal(barrier, inc=1, device_id=device, device_id_type=MESH)
    pl.semaphore_wait(barrier, len(greeted))

    def columns(h):
        return pl.ds(h * (D // 2), D // 2)

    class Gather:
        def __init__(self, name, src, held):
            self.name, self.src, self.held = name, src, held

        def start(self):
            for k in range(2):
                for sign, step in ((0, 1), (1, -1)):
                    h = k if sign == 0 else 1 - k
                    here = self.held.at[g, :, columns(h)]
                    send((self.name, sign, h), self.src.at[:, columns(h)], here, at_y(step))
            send((self.name, "c"), self.src, self.held.at[g], at_y(0, True))
            self.held[pl.ds(g, 1)] = self.src[...][None]

        def forward(self):
            for k in range(2):
                for sign, step in ((0, 1), (1, -1)):
                    h = k if sign == 0 else 1 - k
                    block = member(-step, False)
                    piece = self.held.at[block, :, columns(h)]
                    receive((self.name, sign, h), piece)
                    if k == 0:
                        send((self.name, "far"), piece, piece, at_y(step))
                    else:
                        whole = self.held.at[block]
                        send((self.name, "c"), whole, whole, at_y(0, True))

        def forward_far(self):
            whole = self.held.at[member(2, False)]
            receive((self.name, "far"), whole)
            send((self.name, "c"), whole, whole, at_y(0, True))

        def finish(self):
            receive((self.name, "c"), self.held.at[pl.ds(0, NY)])

    class Near:
        def __init__(self, name, src, held):
            self.name, self.src, self.held = name, src, held

        def start(self):
            for step in (2, 1, 3):
                send((self.name, step), self.src, self.held.at[g], at_y(step))
            send((self.name, "c"), self.src, self.held.at[g], at_y(0, True))
            self.held[pl.ds(g, 1)] = self.src[...][None]

        def forward(self):
            for step in (1, 3, 2):
                block = self.held.at[member(-step, False)]
                receive((self.name, step), block)
                send((self.name, "c"), block, block, at_y(0, True))

        def finish(self):
            receive((self.name, "c"), self.held.at[pl.ds(0, NY)])

    q_gather = Near("q", qh, hq)
    p_gather = [Gather("p%d" % h, ph.at[pl.ds(h * PC, PC)], hp.at[h]) for h in range(2)]

    far = NZ // 2
    leap = far // 2

    def halved(sign):
        return range(sign * SUBS // 2, (sign + 1) * SUBS // 2)

    def z_piece(sign, distance, j):
        block = (z - (1 - 2 * sign) * distance + 2 * NZ) % NZ
        return qall.at[block, pl.ds(j * SUB, SUB)]

    def z_hop(here, there):
        for j in range(SUBS):
            for sign in range(2):
                if there < far or j in halved(sign):
                    piece = z_piece(sign, here, j)
                    if here > 0:
                        receive(("z", sign, here, j), piece)
                    target = at_z((1 - 2 * sign) * (there - here))
                    send(("z", sign, there, j), piece, piece, target, "z")

    def z_step(s):
        if s == 0:
            z_hop(0, 1)
            z_hop(0, leap)
        else:
            if s + 1 < leap:
                z_hop(s, s + 1)
            z_hop(leap + s - 1, leap + s)
        if s == leap:
            for j in range(SUBS):
                for sign in range(2):
                    receive(("z", sign, leap - 1, j), z_piece(sign, leap - 1, j))

    def z_finish():
        for j in range(SUBS):
            for sign in range(2):
                distance = far if j in halved(sign) else far - 1
                receive(("z", sign, distance, j), z_piece(sign, distance, j))
        departures["z"] = qall.at[pl.ds(0, NZ - 1)]

    def x_piece(block, h, half):
        return pall.at[block, pl.ds(h * HALF + half * (HALF // 2), HALF // 2)]

    def x_start(h):
        for k in range(2):
            for sign in range(2):
                half = k if sign == 0 else 1 - k
                piece = x_piece(x, h, half)
                send(("x", h, sign, half), piece, piece, at_x(1 - 2 * sign))

    def x_forward(h):
        for sign in range(2):
            step = 1 - 2 * sign
            piece = x_piece((x - step + NX) % NX, h, sign)
            receive(("x", h, sign, sign), piece)
            send(("x", h, "far"), piece, piece, at_x(step))

    def x_finish(h):
        for sign in range(2):
            step = 1 - 2 * sign
            receive(("x", h, sign, 1 - sign), x_piece((x - step + NX) % NX, h, 1 - sign))
        receive(("x", h, "far"), pall.at[(x + 2) % NX, pl.ds(h * HALF, HALF)])

    def find_slots():
        pieces = []
        for a in range(NZ):
            start = pl.multiple_of(a * NX * GQ + (x // 2) * 2 * GQ, 2 * GQ)
            pieces.append(idv[:, pl.ds(start, 2 * GQ)].astype(F32))
        turned = jnp.concatenate(pieces, axis=0).T
        odd = (x % 2).astype(F32)
        ids = (turned[:GQ] * (1.0 - odd) + turned[GQ:] * odd).astype(I32)
        owner = (ids >> 8) - z * NX
        place = ids & 255
        place = ((place >> 4) & 1) * HALF + (place >> 5) * PC + (place & 15)
        mine = jnp.concatenate([(owner == o).astype(F32) for o in range(NX)], axis=0)
        picked = mine.astype(BF16)
        shape = (NX * GQ, NZ * NEG)
        i, j = iota(shape, 0), iota(shape, 1)
        before = ((i // GQ == j // GQ) & (j < i)).astype(F32).astype(BF16)
        same = i // NEG == j // NEG
        ahead = (same & (i < j)).astype(F32).astype(BF16)
        row_sums = nn(before, picked).astype(BF16)
        rank = nn(row_sums, same.astype(F32).astype(BF16)) + nn(picked, ahead)
        slot = mine * (rank + ((i // GQ) * CAP + 1).astype(F32))
        slot = slot[:GQ] + slot[GQ : 2 * GQ] + slot[2 * GQ : 3 * GQ] + slot[3 * GQ :]
        both = slot.astype(I32) * 256 + place
        both = jnp.where(slot > 0.0, both, 0)
        for a in range(NZ):
            code[a] = both[:, a * NEG : (a + 1) * NEG]

    def fill_slots(first, count):
        def one(a, carry):
            block = code[a]
            lane = iota((GQ, SLOTS), 1) + 1
            hit = jnp.zeros((GQ, SLOTS), F32)
            spot = jnp.zeros((GQ, SLOTS), I32)
            for k in range(NEG):
                column = jnp.broadcast_to(block[:, k : k + 1], (GQ, SLOTS))
                found = (column >> 8) == lane
                hit = jnp.where(found, 1.0, hit)
                spot = jnp.where(found, column & 255, spot)
            hits[a] = hit
            fill[pl.ds(a, 1), :] = jnp.sum(hit, axis=0, keepdims=True)
            row = jnp.sum(spot.astype(F32), axis=0, keepdims=True)
            column = to_column(row, eye(SLOTS, SLOTS)).astype(I32)
            chosen = (iota((SLOTS, GP), 1) == column).astype(F32).astype(BF16)
            for o in range(NX):
                one_hot[o, a] = chosen[o * CAP : (o + 1) * CAP]
            return carry

        lax.fori_loop(first, first + count, one, 0)

    def share(name, pay, got):
        for step, other in others:
            send(name, pay, got.at[g], at_y(step, other))

    def collect(name, pay, got):
        got[pl.ds(g, 1)] = pay[...][None]
        receive(name, got.at[pl.ds(0, NG - 1)])
        total = got[0]
        for i in range(1, NG):
            total = total + got[i]
        return total

    def project_passages(h):
        rows = hp[h].reshape(HALF, D)
        pall[pl.ds(x, 1), h * HALF : (h + 1) * HALF] = nn(rows, wv[...]).astype(BF16)[None]
        x_start(h)

    eye_q, eye_s = eye(GQ, SLOTS), eye(SLOTS, SLOTS)
    p_first, p_second = p_gather

    q_gather.start()
    p_first.start()
    id_copy.wait()
    find_slots()
    q_gather.forward()
    p_second.start()
    fill_slots(0, 4)
    p_first.forward()
    q_gather.finish()
    rows = hq[...].astype(F32).reshape(GQ, D).astype(BF16)
    projected = jnp.zeros((GQ, COLS), F32)
    for k, one in enumerate(w_copies):
        one.wait()
        part = slice(k * COLS, (k + 1) * COLS)
        projected = projected + nn(rows[:, part], wv[part, :])
    qall[pl.ds(z, 1)] = projected.astype(BF16)[None]
    z_step(0)
    p_second.forward()
    p_first.forward_far()
    fill_slots(4, 4)
    p_first.finish()
    project_passages(0)
    z_step(1)
    p_second.forward_far()
    fill_slots(8, 2)
    p_second.finish()
    project_passages(1)
    z_step(2)

    own_q, own_p = qall[z], pall[x]
    for h in range(2):
        part = own_p[h * HALF : (h + 1) * HALF]
        payn[h : h + 1] = jnp.sum(nt(part, part) * eye_s, axis=0, keepdims=True)
    own_q32 = own_q.astype(F32)
    payn[2:3] = to_row(jnp.sum(own_q32 * own_q32, axis=1, keepdims=True), eye_q)
    payn[3:] = jnp.zeros((payn.shape[0] - 3, SLOTS), F32)
    share("n", payn, gotn)

    inner = nt(own_q, own_p)
    pay1[0:GQ] = inner[:, :SLOTS]
    pay1[GQ:] = inner[:, SLOTS:]
    share("s1", pay1, got1)
    x_forward(0)
    z_step(3)
    fill_slots(10, 4)
    sums = collect("n", payn, gotn)
    square_p = jnp.concatenate([sums[0:1], sums[1:2]], axis=1)
    square_q = to_column(sums[2:3], eye_q)
    nz_out[...] = sums[2:3]
    nx_out[...] = square_p
    nz_in[pl.ds(z, 1)] = sums[2:3][None]
    nx_in[pl.ds(x, 1)] = square_p[None]
    for s in range(1, NX):
        send("nx", nx_out, nx_in.at[x], at_x(s))
    for s in range(1, NZ):
        send("nz", nz_out, nz_in.at[z], at_z(s))
    x_forward(1)
    z_step(4)
    fill_slots(14, 2)
    x_finish(0)
    x_finish(1)

    for o in range(NX):
        chosen = nn(one_hot[o].reshape(NZ * CAP, GP), pall[o])
        prow[:, o * CAP : (o + 1) * CAP, :] = chosen.astype(BF16).reshape(NZ, CAP, COLS)

    def by_groups(one, first=0, count=NZ, width=4):
        def some(i, carry):
            for k in range(width):
                one(first + i * width + k)
            return carry

        lax.fori_loop(0, count // width, some, 0)

    def pair_products(step):
        a = (z + step + 2 * NZ) % NZ
        products = nt(qall[a], prow[a])
        pay2[pl.ds(a, 1), :] = jnp.sum(products * hits[a], axis=0, keepdims=True)

    by_groups(pair_products, 2 - NZ // 2, NZ - 4)
    z_finish()
    for step in (NZ // 2 - 2, NZ // 2 - 1, NZ // 2, NZ // 2 + 1):
        pair_products(step)
    share("s2", pay2, got2)

    receive("nx", nx_in.at[pl.ds(0, NX - 1)])
    receive("nz", nz_in.at[pl.ds(0, NZ - 1)])

    depart()

    def slot_norms(a):
        column = to_column(nz_in[a], eye(GQ, SLOTS))
        sl_q[pl.ds(a, 1), :] = jnp.sum(hits[a] * column, axis=0, keepdims=True)
        columns = [
            jnp.sum(one_hot[o, a].astype(F32) * nx_in[o], axis=1, keepdims=True) for o in range(NX)
        ]
        sl_p[pl.ds(a, 1), :] = to_row(jnp.concatenate(columns, axis=0), eye(SLOTS, SLOTS))

    by_groups(slot_norms)

    sums = collect("s1", pay1, got1)
    inner = jnp.concatenate([sums[0:GQ], sums[GQ : 2 * GQ]], axis=1)
    norm = jnp.sqrt(square_q + EPSILON) * jnp.sqrt(square_p + EPSILON)
    cosine = inner / norm
    weight = jnp.exp((cosine - 1.0) / TEMPERATURE)
    weight_sum = jnp.sum(weight, axis=1, keepdims=True)
    spot = iota((GQ, GP), 1)
    passage = ((spot >> 4) & 7) * PR + (spot >> 7) * PC + (spot & 15)
    positive = (passage == iota((GQ, GP), 0) * 4).astype(F32)

    inner_slot = collect("s2", pay2, got2)
    square_slot_p = sl_p[...]
    norm_slot_q = jnp.sqrt(sl_q[...] + EPSILON)
    norm_slot_p = jnp.sqrt(square_slot_p + EPSILON)
    cosine_slot = inner_slot / (norm_slot_q * norm_slot_p)
    weight_slot = jnp.exp((cosine_slot - 1.0) / TEMPERATURE) * fill[...]
    sum2[0:NZ] = weight_slot
    sum2[NZ:] = weight_slot * cosine_slot
    w_p[...] = weight_slot / norm_slot_p
    k_c[...] = weight_slot / (norm_slot_q * norm_slot_p) / TEMPERATURE
    r_c[...] = weight_slot * cosine_slot / (square_slot_p + EPSILON) / TEMPERATURE

    def query_terms(a):
        coefficient = (hits[a] * w_p[pl.ds(a, 1), :]).astype(BF16)
        return nn(coefficient, prow[a])

    def zr_hop(here, there):
        for sign in range(2):
            step = 1 - 2 * sign
            terms = query_terms((z + step * here + NZ) % NZ)
            for j in range(SUBS):
                if here == far and j not in halved(sign):
                    continue
                value = terms[j * SUB : (j + 1) * SUB]
                if here not in (far, leap - 1) and (here < far - 1 or j in halved(sign)):
                    receive(("zr", sign, here + 1, j), zin.at[sign, here, j])
                    value = value + zin[sign, here, j].astype(F32)
                zout[sign, here - 1, j] = value.astype(BF16)
                target = zin.at[sign, here - 1, j]
                send(("zr", sign, here, j), zout.at[sign, here - 1, j], target, at_z(step * (here - there)), "zr")

    def zr_step(s):
        here = far - s
        zr_hop(here, here - 1 if here > leap else 0)
        if s < leap - 1:
            zr_hop(leap - 1 - s, leap - 2 - s)

    def eye_at(second):
        return (iota((GQ, SLOTS), 1) == iota((GQ, SLOTS), 0) + GQ * second).astype(F32)

    def partial_totals(i):
        row = jnp.zeros((1, SLOTS), F32)
        for second in range(2):
            a = i + second * (NZ // 2)
            column = jnp.sum(hits[a] * sum2[pl.ds(a, 1), :], axis=1, keepdims=True)
            row = row + to_row(column, eye_at(second))
        t_out[pl.ds(i, 1), :] = row

    by_groups(partial_totals, 0, NZ // 2)
    own_row, own_eye = pl.ds(z % (NZ // 2), 1), eye_at(z // (NZ // 2))
    t_out[own_row, :] = t_out[own_row, :] + to_row(weight_sum, own_eye)
    t_in[pl.ds(z, 1)] = t_out[...][None]
    for s in range(1, NZ):
        send("t", t_out, t_in.at[z], at_z(s))
    zr_step(0)

    def turn_terms(a):
        turned_k[a] = (hits[a] * k_c[pl.ds(a, 1), :]).T.astype(BF16)

    by_groups(turn_terms)
    zr_step(1)
    for o in range(NX):
        turned_hot[o] = one_hot[o].reshape(NZ * CAP, GP).astype(F32).T.astype(BF16)

    receive("t", t_in.at[pl.ds(0, NZ - 1)])
    totals = t_in[0]
    for i in range(1, NZ):
        totals = totals + t_in[i]
    inv[...] = 1.0 / totals

    def passage_terms(a):
        column = to_column(inv[pl.ds(a % (NZ // 2), 1), :], eye_at(a // (NZ // 2)))
        scaled = (qall[a].astype(F32) * column).astype(BF16)
        shares = jnp.sum(hits[a] * column, axis=0, keepdims=True) * r_c[pl.ds(a, 1), :]
        pulls = (eye(SLOTS, SLOTS) * (-shares)).astype(BF16)
        lhs = jnp.concatenate([pulls, turned_k[a]], axis=1)
        terms = nn(lhs, jnp.concatenate([prow[a], scaled], axis=0)).astype(BF16)
        for o in range(NX):
            cq[o, a] = terms[o * CAP : (o + 1) * CAP]

    by_groups(passage_terms, 0, NZ // 2)
    zr_step(2)
    by_groups(passage_terms, NZ // 2, NZ // 2)
    zr_step(3)

    def passage_sums(step):
        o = (x + step + NX) % NX
        gp[o] = nn(turned_hot[o], cq[o].reshape(NZ * CAP, COLS))

    def xr_rows(h, half):
        return slice(h * HALF + half * (HALF // 2), h * HALF + (half + 1) * (HALF // 2))

    def xr_start(h):
        for sign in range(2):
            xout[h, 0, sign] = gp[(x + 2) % NX, xr_rows(h, sign)].astype(BF16)
            send(("xr", h, sign, "far"), xout.at[h, 0, sign], xhalf.at[h, sign], at_x(1 - 2 * sign))

    def xr_own(h):
        for sign in range(2):
            near = (x + 1 - 2 * sign + NX) % NX
            xout[h, 1 + sign, 1 - sign] = gp[near, xr_rows(h, 1 - sign)].astype(BF16)
            there = xfull.at[h, sign, 1 - sign]
            send(("xr", h), xout.at[h, 1 + sign, 1 - sign], there, at_x(1 - 2 * sign))

    def xr_forward(h):
        for sign in range(2):
            near = (x + 1 - 2 * sign + NX) % NX
            receive(("xr", h, sign, "far"), xhalf.at[h, sign])
            merged = gp[near, xr_rows(h, sign)] + xhalf[h, sign].astype(F32)
            xout[h, 1 + sign, sign] = merged.astype(BF16)
            there = xfull.at[h, sign, sign]
            send(("xr", h), xout.at[h, 1 + sign, sign], there, at_x(1 - 2 * sign))

    def xr_finish(h):
        receive(("xr", h), xfull.at[h])
        value = gp[x, h * HALF : (h + 1) * HALF]
        full = xfull[h].reshape(2, HALF, COLS)
        return value + full[0].astype(F32) + full[1].astype(F32)

    class Scatter:
        def __init__(self, name, rows, part, core, out, half, full):
            self.name, self.rows = name, rows
            self.part, self.core, self.out, self.half, self.full = part, core, out, half, full
            self.places = [(y + step) % NY for step in (2, 1, 3, 0)]

        def part_out(self, block, columns):
            block = block.reshape(NY, NC, self.rows, 512)
            for k in range(NC):
                self.part[k, :, :, columns] = block[:, k].astype(BF16)

        def to_core(self):
            for i, place in enumerate(self.places):
                there = self.core.at[place]
                send((self.name, "c", i), self.part.at[1 - c, place], there, at_y(0, True))

        def arrive(self, i):
            receive((self.name, "c", i), self.core.at[self.places[i]])

        def both(self, i, h):
            place = self.places[i]
            cut = slice(h * (D // 2), (h + 1) * (D // 2))
            return self.part[c, place, :, cut].astype(F32) + self.core[place, :, cut].astype(F32)

        def start(self):
            self.arrive(0)
            for sign in range(2):
                self.out[0, sign] = self.both(0, sign).astype(BF16)
                there = self.half.at[sign]
                send((self.name, "far", sign), self.out.at[0, sign], there, at_y(1 - 2 * sign))
            for sign in range(2):
                self.arrive(1 + sign)
                self.out[1 + sign, 1 - sign] = self.both(1 + sign, 1 - sign).astype(BF16)
                there = self.full.at[sign, 1 - sign]
                send((self.name, "full"), self.out.at[1 + sign, 1 - sign], there, at_y(1 - 2 * sign))

        def forward(self):
            for sign in range(2):
                merged = self.both(1 + sign, sign)
                receive((self.name, "far", sign), self.half.at[sign])
                self.out[1 + sign, sign] = (merged + self.half[sign].astype(F32)).astype(BF16)
                there = self.full.at[sign, sign]
                send((self.name, "full"), self.out.at[1 + sign, sign], there, at_y(1 - 2 * sign))

        def finish(self, out):
            self.arrive(3)
            own = [self.both(3, h) for h in range(2)]
            receive((self.name, "full"), self.full)
            for h in range(2):
                total = own[h] + self.full[0, h].astype(F32) + self.full[1, h].astype(F32)
                out[:, h * (D // 2) : (h + 1) * (D // 2)] = total.astype(BF16)

    class NearScatter(Scatter):
        def start(self):
            for i, step in enumerate((2, 1, 3)):
                self.arrive(i)
                for h in range(2):
                    self.out[i, h] = self.both(i, h).astype(BF16)
                send((self.name, "near"), self.out.at[i], self.full.at[i], at_y(step))

        def finish(self, out):
            self.arrive(3)
            own = [self.both(3, h) for h in range(2)]
            receive((self.name, "near"), self.full)
            for h in range(2):
                total = own[h] + self.full[0, h].astype(F32)
                total = total + self.full[1, h].astype(F32) + self.full[2, h].astype(F32)
                out[:, h * (D // 2) : (h + 1) * (D // 2)] = total.astype(BF16)

    def project_back(scatters, downs):
        down = jnp.concatenate(downs, axis=0)

        def one(i, carry):
            columns = pl.ds(pl.multiple_of(i * 512, 512), 512)
            block = nt(down, wv[columns, :])
            first = 0
            for scatter in scatters:
                count = NG * scatter.rows
                scatter.part_out(block[first : first + count], columns)
                first += count
            return carry

        lax.fori_loop(0, D // 512, one, 0)
        for scatter in scatters:
            scatter.to_core()

    q_scatter = NearScatter("Q", QR, qpart, qcore, qout, None, qfull)
    p_scatter = [
        Scatter("P%d" % h, PC, ppart.at[h], pcore.at[h], pout.at[h], phalf.at[h], pfull.at[h])
        for h in range(2)
    ]

    passage_sums(2)
    xr_start(0)
    xr_start(1)
    passage_sums(1)
    passage_sums(-1)
    xr_own(0)
    xr_own(1)
    zr_step(4)
    passage_sums(0)
    def partial_radials(a):
        column = jnp.sum(hits[a] * sum2[pl.ds(NZ + a, 1), :], axis=1, keepdims=True)
        r_out[pl.ds(a, 1)] = to_row(column, eye(GQ, SLOTS))[None]

    by_groups(partial_radials)
    r_in[pl.ds(z, 1)] = r_out[pl.ds(z, 1)]
    for s in range(1, NZ):
        send("r", r_out.at[(z + s) % NZ], r_in.at[z], at_z(s))


    total = 1.0 / to_column(inv[own_row, :], own_eye)
    inverse = 1.0 / total
    loss = jnp.log(total) + (1.0 - jnp.sum(positive * cosine, axis=1, keepdims=True)) / TEMPERATURE
    mine = (iota((GQ, SLOTS), 0) == g * QR + iota((GQ, SLOTS), 1)).astype(F32)
    loss_out[...] = jnp.sum(mine * loss, axis=0, keepdims=True)
    slope = (weight * inverse - positive) / TEMPERATURE
    pull = slope * cosine
    radial_p = jnp.sum(pull, axis=0, keepdims=True) / (square_p + EPSILON)
    coefficient = (slope / norm).astype(BF16)
    group_p = tn(coefficient, own_q)
    xr_forward(0)
    xr_forward(1)
    down_p = []
    eye_p = eye(HALF, HALF)
    for h in range(2):
        column = to_column(radial_p[:, h * HALF : (h + 1) * HALF], eye_p)
        rows = slice(h * HALF, (h + 1) * HALF)
        down_p.append(group_p[rows] - column * own_p[rows].astype(F32))
    receive("r", r_in.at[pl.ds(0, NZ - 1)])
    radials = r_in[0]
    for i in range(1, NZ):
        radials = radials + r_in[i]
    radial_slots = to_column(radials, eye_q) * inverse / TEMPERATURE
    radial_q = jnp.sum(pull, axis=1, keepdims=True) + radial_slots
    group_q = nn(coefficient, own_p) - (radial_q / (square_q + EPSILON)) * own_q32
    own_terms = query_terms(z)

    pieces = []
    for j in range(SUBS):
        piece = own_terms[j * SUB : (j + 1) * SUB]
        for sign in range(2):
            for here in (1, leap):
                receive(("zr", sign, here, j), zin.at[sign, here - 1, j])
                piece = piece + zin[sign, here - 1, j].astype(F32)
        pieces.append(piece)
    departures["zr"] = qall.at[pl.ds(0, NZ - 1)]
    factor = inverse / jnp.sqrt(square_q + EPSILON) / TEMPERATURE
    down_q = (group_q + jnp.concatenate(pieces, axis=0) * factor).astype(BF16)
    project_back([q_scatter], [down_q])
    project_back([p_scatter[0]], [(xr_finish(0) + down_p[0]).astype(BF16)])
    second_p = (xr_finish(1) + down_p[1]).astype(BF16)
    q_scatter.start()
    project_back([p_scatter[1]], [second_p])
    p_scatter[0].start()
    p_scatter[1].start()
    p_scatter[0].forward()
    p_scatter[1].forward()
    q_scatter.finish(qg_out)
    p_scatter[0].finish(pg_out.at[0:PC])
    p_scatter[1].finish(pg_out.at[PC:PR])
    depart()
    assert not departures
    assert len(names) <= CHANNELS


def place_outputs(loss, query_grad, passage_grad, loss_out, query_out, passage_out):
    loss_out[...] = loss[0, :QR]
    query_out[...] = query_grad[...]
    passage_out[...] = passage_grad[...]


def per_device(query_hidden, passage_hidden, projection, negative_ids):
    vmem = pl.BlockSpec(memory_space=pltpu.VMEM)
    hbm = pl.BlockSpec(memory_space=pl.ANY)
    v = pltpu.VMEM
    loss, query_grad, passage_grad = pl.pallas_call(
        kernel,
        out_shape=(
            jax.ShapeDtypeStruct((1, SLOTS), F32),
            jax.ShapeDtypeStruct((QR, D), BF16),
            jax.ShapeDtypeStruct((PR, D), BF16),
        ),
        in_specs=[vmem, vmem, hbm, hbm],
        out_specs=(vmem, vmem, vmem),
        scratch_shapes=[
            v((D, COLS), BF16),
            v((NEG, NZ * NX * GQ), I32),
            v((NG, QR, D), BF16),
            v((2, NG, PC, D), BF16),
            v((NZ, GQ, COLS), BF16),
            v((NX, GP, COLS), BF16),
            v((NZ, GQ, NEG), I32),
            v((NZ, GQ, SLOTS), F32),
            v((NX, NZ, CAP, GP), BF16),
            v((NZ, SLOTS, COLS), BF16),
            v((2 * GQ, SLOTS), F32),
            v((NG, 2 * GQ, SLOTS), F32),
            v((8, SLOTS), F32),
            v((NG, 8, SLOTS), F32),
            v((1, SLOTS), F32),
            v((NZ, 1, SLOTS), F32),
            v((1, GP), F32),
            v((NX, 1, GP), F32),
            v((NZ, SLOTS), F32),
            v((NZ, SLOTS), F32),
            v((NZ, SLOTS), F32),
            v((NG, NZ, SLOTS), F32),
            v((2 * NZ, SLOTS), F32),
            v((NZ, SLOTS), F32),
            v((NZ, SLOTS), F32),
            v((NZ, SLOTS), F32),
            v((NZ, SLOTS), F32),
            v((NZ // 2, SLOTS), F32),
            v((NZ, NZ // 2, SLOTS), F32),
            v((NZ // 2, SLOTS), F32),
            v((NZ, 1, SLOTS), F32),
            v((NZ, 1, SLOTS), F32),
            v((2, NZ // 2, SUBS, SUB, COLS), BF16),
            v((2, NZ // 2, SUBS, SUB, COLS), BF16),
            v((NZ, SLOTS, GQ), BF16),
            v((NX, GP, NZ * CAP), BF16),
            v((NX, NZ, CAP, COLS), BF16),
            v((NX, GP, COLS), F32),
            v((2, 3, 2, HALF // 2, COLS), BF16),
            v((2, 2, HALF // 2, COLS), BF16),
            v((2, 2, 2, HALF // 2, COLS), BF16),
            v((NC, NY, QR, D), BF16),
            v((NY, QR, D), BF16),
            v((3, 2, QR, D // 2), BF16),
            v((3, 2, QR, D // 2), BF16),
            v((2, NC, NY, PC, D), BF16),
            v((2, NY, PC, D), BF16),
            v((2, 3, 2, PC, D // 2), BF16),
            v((2, 2, PC, D // 2), BF16),
            v((2, 2, 2, PC, D // 2), BF16),
            pltpu.SemaphoreType.DMA((10,)),
            pltpu.SemaphoreType.DMA((CHANNELS,)),
            pltpu.SemaphoreType.DMA((CHANNELS,)),
        ],
        compiler_params=pltpu.CompilerParams(
            collective_id=0, has_side_effects=True, vmem_limit_bytes=56 * 1024 * 1024
        ),
    )(query_hidden, passage_hidden, projection, negative_ids.T)
    return pl.pallas_call(
        place_outputs,
        out_shape=(
            jax.ShapeDtypeStruct((QR,), F32),
            jax.ShapeDtypeStruct((QR, D), BF16),
            jax.ShapeDtypeStruct((PR, D), BF16),
        ),
        in_specs=[vmem, vmem, vmem],
        out_specs=(vmem, vmem, vmem),
    )(loss, query_grad, passage_grad)


def solution(mesh):
    in_specs = (P(("dp", "group"), None), P(("dp", "group"), None), P(None, "group"), P())
    out_specs = (P(("dp", "group")), P(("dp", "group"), None), P(("dp", "group"), None))
    return jax.shard_map(
        per_device, mesh=mesh, in_specs=in_specs, out_specs=out_specs, check_vma=False
    )
```

```python
import jax
import jax.numpy as jnp
from jax import lax
from jax.experimental import pallas as pl
from jax.experimental.pallas import tpu as pltpu
from jax.sharding import PartitionSpec as P

TEMPERATURE = 0.05
EPSILON = 1e-06
MESH = pl.DeviceIdType.MESH
F32, BF16, I32 = jnp.float32, jnp.bfloat16, jnp.int32

NZ, NX, NY, NC = 16, 4, 4, 2
NG = NY * NC
D = 4096
COLS = D // NG
QR, PR, PC = 8, 32, 16
GQ, GP = QR * NG, PR * NG
HALF = GP // 2
NEG, CAP = 16, 32
SLOTS = NX * CAP
CHANNELS = 256
SUBS = 2
SUB = GQ // SUBS


def nn(a, b):
    return lax.dot_general(a, b, (((1,), (0,)), ((), ())), preferred_element_type=F32)


def nt(a, b):
    return lax.dot_general(a, b, (((1,), (1,)), ((), ())), preferred_element_type=F32)


def tn(a, b):
    return lax.dot_general(a, b, (((0,), (0,)), ((), ())), preferred_element_type=F32)


def iota(shape, dim):
    return lax.broadcasted_iota(I32, shape, dim)


def eye(rows, columns):
    return (iota((rows, columns), 0) == iota((rows, columns), 1)).astype(F32)


def to_row(column, identity):
    return jnp.sum(identity * column, axis=0, keepdims=True)


def to_column(row, identity):
    return jnp.sum(identity * row, axis=1, keepdims=True)


def kernel(
    qh, ph, weight_hbm, ids_hbm,
    loss_out, qg_out, pg_out,
    wv, idv, hq, hp, qall, pall, code, hits, one_hot, prow,
    pay1, got1, payn, gotn, nz_out, nz_in, nx_out, nx_in, sl_q, sl_p,
    pay2, got2, sum2, fill, w_p, k_c, r_c, t_out, t_in, inv, r_out, r_in,
    zout, zin, turned_k, turned_hot, cq, gp, xout, xhalf, xfull,
    qpart, qcore, qout, qfull, ppart, pcore, pout, phalf, pfull,
    local_sem, send_sem, recv_sem,
):
    dp, g = lax.axis_index("dp"), lax.axis_index("group")
    z, x = dp // NX, dp % NX
    y, c = g // NC, g % NC

    def at_z(step):
        return (((z + step + 2 * NZ) % NZ) * NX + x, g)

    def at_x(step):
        return (z * NX + (x + step + NX) % NX, g)

    def member(step, other):
        return ((y + step + NY) % NY) * NC + (1 - c if other else c)

    def at_y(step, other=False):
        return (dp, member(step, other))

    others = [(s, o) for s in (0, 1, 2, 3) for o in (False, True) if (s, o) != (0, False)]

    names, departures = {}, {}

    def channel(name):
        return names.setdefault(name, len(names))

    def copy(name, group, src, dst, device):
        return pltpu.make_async_remote_copy(
            src_ref=src, dst_ref=dst, send_sem=send_sem.at[channel(("from", group))],
            recv_sem=recv_sem.at[channel(name)], device_id=device, device_id_type=MESH,
        )

    def send(name, src, dst, device, group=None):
        group = name if group is None else group
        departures.setdefault(group, None)
        copy(name, group, src, dst, device).start()

    def receive(name, dst):
        if name in departures:
            departures[name] = dst
        copy(name, name, dst, dst, at_x(1)).wait_recv()

    def depart():
        for group, ref in list(departures.items()):
            if ref is not None:
                copy(group, group, ref, ref, at_x(1)).wait_send()
                del departures[group]

    w_copies = []
    for k in range(8):
        rows = pl.ds(k * COLS, COLS)
        w_copies.append(pltpu.make_async_copy(weight_hbm.at[rows], wv.at[rows], local_sem.at[2 + k]))
        w_copies[-1].start()
    id_copy = pltpu.make_async_copy(ids_hbm, idv, local_sem.at[1])
    id_copy.start()
    barrier = pltpu.get_barrier_semaphore()
    greeted = [at_z(s) for s in range(1, NZ)] + [at_x(s) for s in range(1, NX)] + [at_y(*o) for o in others]
    for device in greeted:
        pl.semaphore_signal(barrier, inc=1, device_id=device, device_id_type=MESH)
    pl.semaphore_wait(barrier, len(greeted))

    def columns(h):
        return pl.ds(h * (D // 2), D // 2)

    class Gather:
        def __init__(self, name, src, held):
            self.name, self.src, self.held = name, src, held

        def start(self):
            for k in range(2):
                for sign, step in ((0, 1), (1, -1)):
                    h = k if sign == 0 else 1 - k
                    here = self.held.at[g, :, columns(h)]
                    send((self.name, sign, h), self.src.at[:, columns(h)], here, at_y(step))
            send((self.name, "c"), self.src, self.held.at[g], at_y(0, True))
            self.held[pl.ds(g, 1)] = self.src[...][None]

        def forward(self):
            for k in range(2):
                for sign, step in ((0, 1), (1, -1)):
                    h = k if sign == 0 else 1 - k
                    block = member(-step, False)
                    piece = self.held.at[block, :, columns(h)]
                    receive((self.name, sign, h), piece)
                    if k == 0:
                        send((self.name, "far"), piece, piece, at_y(step))
                    else:
                        whole = self.held.at[block]
                        send((self.name, "c"), whole, whole, at_y(0, True))

        def forward_far(self):
            whole = self.held.at[member(2, False)]
            receive((self.name, "far"), whole)
            send((self.name, "c"), whole, whole, at_y(0, True))

        def finish(self):
            receive((self.name, "c"), self.held.at[pl.ds(0, NY)])

    class Near:
        def __init__(self, name, src, held):
            self.name, self.src, self.held = name, src, held

        def start(self):
            for step in (2, 1, 3):
                send((self.name, step), self.src, self.held.at[g], at_y(step))
            send((self.name, "c"), self.src, self.held.at[g], at_y(0, True))
            self.held[pl.ds(g, 1)] = self.src[...][None]

        def forward(self):
            for step in (1, 3, 2):
                block = self.held.at[member(-step, False)]
                receive((self.name, step), block)
                send((self.name, "c"), block, block, at_y(0, True))

        def finish(self):
            receive((self.name, "c"), self.held.at[pl.ds(0, NY)])

    q_gather = Near("q", qh, hq)
    p_gather = [Gather("p%d" % h, ph.at[pl.ds(h * PC, PC)], hp.at[h]) for h in range(2)]

    far = NZ // 2
    leap = far // 2

    def halved(sign):
        return range(sign * SUBS // 2, (sign + 1) * SUBS // 2)

    def z_piece(sign, distance, j):
        block = (z - (1 - 2 * sign) * distance + 2 * NZ) % NZ
        return qall.at[block, pl.ds(j * SUB, SUB)]

    def z_hop(here, there):
        for j in range(SUBS):
            for sign in range(2):
                if there < far or j in halved(sign):
                    piece = z_piece(sign, here, j)
                    if here > 0:
                        receive(("z", sign, here, j), piece)
                    target = at_z((1 - 2 * sign) * (there - here))
                    send(("z", sign, there, j), piece, piece, target, "z")

    def z_step(s):
        if s == 0:
            z_hop(0, 1)
            z_hop(0, leap)
        else:
            if s + 1 < leap:
                z_hop(s, s + 1)
            z_hop(leap + s - 1, leap + s)
        if s == leap:
            for j in range(SUBS):
                for sign in range(2):
                    receive(("z", sign, leap - 1, j), z_piece(sign, leap - 1, j))

    def z_finish():
        for j in range(SUBS):
            for sign in range(2):
                distance = far if j in halved(sign) else far - 1
                receive(("z", sign, distance, j), z_piece(sign, distance, j))
        departures["z"] = qall.at[pl.ds(0, NZ - 1)]

    def x_piece(block, h, half):
        return pall.at[block, pl.ds(h * HALF + half * (HALF // 2), HALF // 2)]

    def x_start(h):
        for k in range(2):
            for sign in range(2):
                half = k if sign == 0 else 1 - k
                piece = x_piece(x, h, half)
                send(("x", h, sign, half), piece, piece, at_x(1 - 2 * sign))

    def x_forward(h):
        for sign in range(2):
            step = 1 - 2 * sign
            piece = x_piece((x - step + NX) % NX, h, sign)
            receive(("x", h, sign, sign), piece)
            send(("x", h, "far"), piece, piece, at_x(step))

    def x_finish(h):
        for sign in range(2):
            step = 1 - 2 * sign
            receive(("x", h, sign, 1 - sign), x_piece((x - step + NX) % NX, h, 1 - sign))
        receive(("x", h, "far"), pall.at[(x + 2) % NX, pl.ds(h * HALF, HALF)])

    def find_slots():
        pieces = []
        for a in range(NZ):
            start = pl.multiple_of(a * NX * GQ + (x // 2) * 2 * GQ, 2 * GQ)
            pieces.append(idv[:, pl.ds(start, 2 * GQ)].astype(F32))
        turned = jnp.concatenate(pieces, axis=0).T
        odd = (x % 2).astype(F32)
        ids = (turned[:GQ] * (1.0 - odd) + turned[GQ:] * odd).astype(I32)
        owner = (ids >> 8) - z * NX
        place = ids & 255
        place = ((place >> 4) & 1) * HALF + (place >> 5) * PC + (place & 15)
        mine = jnp.concatenate([(owner == o).astype(F32) for o in range(NX)], axis=0)
        picked = mine.astype(BF16)
        shape = (NX * GQ, NZ * NEG)
        i, j = iota(shape, 0), iota(shape, 1)
        before = ((i // GQ == j // GQ) & (j < i)).astype(F32).astype(BF16)
        same = i // NEG == j // NEG
        ahead = (same & (i < j)).astype(F32).astype(BF16)
        row_sums = nn(before, picked).astype(BF16)
        rank = nn(row_sums, same.astype(F32).astype(BF16)) + nn(picked, ahead)
        slot = mine * (rank + ((i // GQ) * CAP + 1).astype(F32))
        slot = slot[:GQ] + slot[GQ : 2 * GQ] + slot[2 * GQ : 3 * GQ] + slot[3 * GQ :]
        both = slot.astype(I32) * 256 + place
        both = jnp.where(slot > 0.0, both, 0)
        for a in range(NZ):
            code[a] = both[:, a * NEG : (a + 1) * NEG]

    def fill_slots(first, count):
        def one(a, carry):
            block = code[a]
            lane = iota((GQ, SLOTS), 1) + 1
            hit = jnp.zeros((GQ, SLOTS), F32)
            spot = jnp.zeros((GQ, SLOTS), I32)
            for k in range(NEG):
                column = jnp.broadcast_to(block[:, k : k + 1], (GQ, SLOTS))
                found = (column >> 8) == lane
                hit = jnp.where(found, 1.0, hit)
                spot = jnp.where(found, column & 255, spot)
            hits[a] = hit
            fill[pl.ds(a, 1), :] = jnp.sum(hit, axis=0, keepdims=True)
            row = jnp.sum(spot.astype(F32), axis=0, keepdims=True)
            column = to_column(row, eye(SLOTS, SLOTS)).astype(I32)
            chosen = (iota((SLOTS, GP), 1) == column).astype(F32).astype(BF16)
            for o in range(NX):
                one_hot[o, a] = chosen[o * CAP : (o + 1) * CAP]
            return carry

        def two(i, carry):
            one(first + 2 * i, carry)
            return one(first + 2 * i + 1, carry)

        lax.fori_loop(0, count // 2, two, 0)

    def share(name, pay, got):
        for step, other in others:
            send(name, pay, got.at[g], at_y(step, other))

    def collect(name, pay, got):
        got[pl.ds(g, 1)] = pay[...][None]
        receive(name, got.at[pl.ds(0, NG - 1)])
        total = got[0]
        for i in range(1, NG):
            total = total + got[i]
        return total

    def project_passages(h):
        rows = hp[h].reshape(HALF, D)
        pall[pl.ds(x, 1), h * HALF : (h + 1) * HALF] = nn(rows, wv[...]).astype(BF16)[None]
        x_start(h)

    eye_q, eye_s = eye(GQ, SLOTS), eye(SLOTS, SLOTS)
    p_first, p_second = p_gather

    q_gather.start()
    p_first.start()
    id_copy.wait()
    find_slots()
    q_gather.forward()
    p_second.start()
    fill_slots(0, 4)
    p_first.forward()
    q_gather.finish()
    rows = hq[...].astype(F32).reshape(GQ, D).astype(BF16)
    projected = jnp.zeros((GQ, COLS), F32)
    for k, one in enumerate(w_copies):
        one.wait()
        part = slice(k * COLS, (k + 1) * COLS)
        projected = projected + nn(rows[:, part], wv[part, :])
    qall[pl.ds(z, 1)] = projected.astype(BF16)[None]
    z_step(0)
    p_second.forward()
    p_first.forward_far()
    fill_slots(4, 4)
    p_first.finish()
    project_passages(0)
    z_step(1)
    p_second.forward_far()
    fill_slots(8, 2)
    p_second.finish()
    project_passages(1)
    z_step(2)

    own_q, own_p = qall[z], pall[x]
    for h in range(2):
        part = own_p[h * HALF : (h + 1) * HALF]
        payn[h : h + 1] = jnp.sum(nt(part, part) * eye_s, axis=0, keepdims=True)
    own_q32 = own_q.astype(F32)
    payn[2:3] = to_row(jnp.sum(own_q32 * own_q32, axis=1, keepdims=True), eye_q)
    payn[3:] = jnp.zeros((payn.shape[0] - 3, SLOTS), F32)
    share("n", payn, gotn)

    inner = nt(own_q, own_p)
    pay1[0:GQ] = inner[:, :SLOTS]
    pay1[GQ:] = inner[:, SLOTS:]
    share("s1", pay1, got1)
    x_forward(0)
    z_step(3)
    fill_slots(10, 4)
    sums = collect("n", payn, gotn)
    square_p = jnp.concatenate([sums[0:1], sums[1:2]], axis=1)
    square_q = to_column(sums[2:3], eye_q)
    nz_out[...] = sums[2:3]
    nx_out[...] = square_p
    nz_in[pl.ds(z, 1)] = sums[2:3][None]
    nx_in[pl.ds(x, 1)] = square_p[None]
    for s in range(1, NX):
        send("nx", nx_out, nx_in.at[x], at_x(s))
    for s in range(1, NZ):
        send("nz", nz_out, nz_in.at[z], at_z(s))
    x_forward(1)
    z_step(4)
    fill_slots(14, 2)
    x_finish(0)
    x_finish(1)

    for o in range(NX):
        chosen = nn(one_hot[o].reshape(NZ * CAP, GP), pall[o])
        prow[:, o * CAP : (o + 1) * CAP, :] = chosen.astype(BF16).reshape(NZ, CAP, COLS)

    def by_groups(one, first=0, count=NZ, width=8):
        def some(i, carry):
            for k in range(width):
                one(first + i * width + k)
            return carry

        lax.fori_loop(0, count // width, some, 0)

    def pair_products(step):
        a = (z + step + 2 * NZ) % NZ
        products = nt(qall[a], prow[a])
        pay2[pl.ds(a, 1), :] = jnp.sum(products * hits[a], axis=0, keepdims=True)

    by_groups(pair_products, 2 - NZ // 2, NZ - 4, 6)
    z_finish()
    for step in (NZ // 2 - 2, NZ // 2 - 1, NZ // 2, NZ // 2 + 1):
        pair_products(step)
    share("s2", pay2, got2)

    receive("nx", nx_in.at[pl.ds(0, NX - 1)])
    receive("nz", nz_in.at[pl.ds(0, NZ - 1)])

    depart()

    def slot_norms(a):
        column = to_column(nz_in[a], eye(GQ, SLOTS))
        sl_q[pl.ds(a, 1), :] = jnp.sum(hits[a] * column, axis=0, keepdims=True)
        columns = [
            jnp.sum(one_hot[o, a].astype(F32) * nx_in[o], axis=1, keepdims=True) for o in range(NX)
        ]
        sl_p[pl.ds(a, 1), :] = to_row(jnp.concatenate(columns, axis=0), eye(SLOTS, SLOTS))

    by_groups(slot_norms)

    sums = collect("s1", pay1, got1)
    inner = jnp.concatenate([sums[0:GQ], sums[GQ : 2 * GQ]], axis=1)
    norm = jnp.sqrt(square_q + EPSILON) * jnp.sqrt(square_p + EPSILON)
    cosine = inner / norm
    weight = jnp.exp((cosine - 1.0) / TEMPERATURE)
    weight_sum = jnp.sum(weight, axis=1, keepdims=True)
    spot = iota((GQ, GP), 1)
    passage = ((spot >> 4) & 7) * PR + (spot >> 7) * PC + (spot & 15)
    positive = (passage == iota((GQ, GP), 0) * 4).astype(F32)

    inner_slot = collect("s2", pay2, got2)
    square_slot_p = sl_p[...]
    norm_slot_q = jnp.sqrt(sl_q[...] + EPSILON)
    norm_slot_p = jnp.sqrt(square_slot_p + EPSILON)
    cosine_slot = inner_slot / (norm_slot_q * norm_slot_p)
    weight_slot = jnp.exp((cosine_slot - 1.0) / TEMPERATURE) * fill[...]
    sum2[0:NZ] = weight_slot
    sum2[NZ:] = weight_slot * cosine_slot
    w_p[...] = weight_slot / norm_slot_p
    k_c[...] = weight_slot / (norm_slot_q * norm_slot_p) / TEMPERATURE
    r_c[...] = weight_slot * cosine_slot / (square_slot_p + EPSILON) / TEMPERATURE

    def query_terms(a):
        coefficient = (hits[a] * w_p[pl.ds(a, 1), :]).astype(BF16)
        return nn(coefficient, prow[a])

    def zr_hop(here, there):
        terms = None
        for sign in range(2):
            step = 1 - 2 * sign
            if here < far or terms is None:
                terms = query_terms((z + step * here + NZ) % NZ)
            for j in range(SUBS):
                if here == far and j not in halved(sign):
                    continue
                value = terms[j * SUB : (j + 1) * SUB]
                if here not in (far, leap - 1) and (here < far - 1 or j in halved(sign)):
                    receive(("zr", sign, here + 1, j), zin.at[sign, here, j])
                    value = value + zin[sign, here, j].astype(F32)
                zout[sign, here - 1, j] = value.astype(BF16)
                target = zin.at[sign, here - 1, j]
                send(("zr", sign, here, j), zout.at[sign, here - 1, j], target, at_z(step * (here - there)), "zr")

    def zr_step(s):
        here = far - s
        zr_hop(here, here - 1 if here > leap else 0)
        if s < leap - 1:
            zr_hop(leap - 1 - s, leap - 2 - s)

    def eye_at(second):
        return (iota((GQ, SLOTS), 1) == iota((GQ, SLOTS), 0) + GQ * second).astype(F32)

    def partial_totals(i):
        row = jnp.zeros((1, SLOTS), F32)
        for second in range(2):
            a = i + second * (NZ // 2)
            column = jnp.sum(hits[a] * sum2[pl.ds(a, 1), :], axis=1, keepdims=True)
            row = row + to_row(column, eye_at(second))
        t_out[pl.ds(i, 1), :] = row

    by_groups(partial_totals, 0, NZ // 2)
    own_row, own_eye = pl.ds(z % (NZ // 2), 1), eye_at(z // (NZ // 2))
    t_out[own_row, :] = t_out[own_row, :] + to_row(weight_sum, own_eye)
    t_in[pl.ds(z, 1)] = t_out[...][None]
    for s in range(1, NZ):
        send("t", t_out, t_in.at[z], at_z(s))
    zr_step(0)

    def turn_terms(a):
        turned_k[a] = (hits[a] * k_c[pl.ds(a, 1), :]).T.astype(BF16)

    by_groups(turn_terms)
    zr_step(1)
    for o in range(NX):
        turned_hot[o] = one_hot[o].reshape(NZ * CAP, GP).astype(F32).T.astype(BF16)

    receive("t", t_in.at[pl.ds(0, NZ - 1)])
    totals = t_in[0]
    for i in range(1, NZ):
        totals = totals + t_in[i]
    inv[...] = 1.0 / totals

    def passage_terms(a):
        column = to_column(inv[pl.ds(a % (NZ // 2), 1), :], eye_at(a // (NZ // 2)))
        scaled = (qall[a].astype(F32) * column).astype(BF16)
        shares = jnp.sum(hits[a] * column, axis=0, keepdims=True) * r_c[pl.ds(a, 1), :]
        pulls = (eye(SLOTS, SLOTS) * (-shares)).astype(BF16)
        lhs = jnp.concatenate([pulls, turned_k[a]], axis=1)
        terms = nn(lhs, jnp.concatenate([prow[a], scaled], axis=0)).astype(BF16)
        for o in range(NX):
            cq[o, a] = terms[o * CAP : (o + 1) * CAP]

    by_groups(passage_terms, 0, NZ // 2)
    zr_step(2)
    by_groups(passage_terms, NZ // 2, NZ // 2)
    zr_step(3)

    def passage_sums(step):
        o = (x + step + NX) % NX
        gp[o] = nn(turned_hot[o], cq[o].reshape(NZ * CAP, COLS))

    def xr_rows(h, half):
        return slice(h * HALF + half * (HALF // 2), h * HALF + (half + 1) * (HALF // 2))

    def xr_start(h):
        for sign in range(2):
            xout[h, 0, sign] = gp[(x + 2) % NX, xr_rows(h, sign)].astype(BF16)
            send(("xr", h, sign, "far"), xout.at[h, 0, sign], xhalf.at[h, sign], at_x(1 - 2 * sign))

    def xr_own(h):
        for sign in range(2):
            near = (x + 1 - 2 * sign + NX) % NX
            xout[h, 1 + sign, 1 - sign] = gp[near, xr_rows(h, 1 - sign)].astype(BF16)
            there = xfull.at[h, sign, 1 - sign]
            send(("xr", h), xout.at[h, 1 + sign, 1 - sign], there, at_x(1 - 2 * sign))

    def xr_forward(h):
        for sign in range(2):
            near = (x + 1 - 2 * sign + NX) % NX
            receive(("xr", h, sign, "far"), xhalf.at[h, sign])
            merged = gp[near, xr_rows(h, sign)] + xhalf[h, sign].astype(F32)
            xout[h, 1 + sign, sign] = merged.astype(BF16)
            there = xfull.at[h, sign, sign]
            send(("xr", h), xout.at[h, 1 + sign, sign], there, at_x(1 - 2 * sign))

    def xr_finish(h):
        receive(("xr", h), xfull.at[h])
        value = gp[x, h * HALF : (h + 1) * HALF]
        full = xfull[h].reshape(2, HALF, COLS)
        return value + full[0].astype(F32) + full[1].astype(F32)

    class Scatter:
        def __init__(self, name, rows, part, core, out, half, full):
            self.name, self.rows = name, rows
            self.part, self.core, self.out, self.half, self.full = part, core, out, half, full
            self.places = [(y + step) % NY for step in (2, 1, 3, 0)]

        def part_out(self, block, columns):
            block = block.reshape(NY, NC, self.rows, 512)
            for k in range(NC):
                self.part[k, :, :, columns] = block[:, k].astype(BF16)

        def to_core(self):
            for i, place in enumerate(self.places):
                there = self.core.at[place]
                send((self.name, "c", i), self.part.at[1 - c, place], there, at_y(0, True))

        def arrive(self, i):
            receive((self.name, "c", i), self.core.at[self.places[i]])

        def both(self, i, h):
            place = self.places[i]
            cut = slice(h * (D // 2), (h + 1) * (D // 2))
            return self.part[c, place, :, cut].astype(F32) + self.core[place, :, cut].astype(F32)

        def start(self):
            self.arrive(0)
            for sign in range(2):
                self.out[0, sign] = self.both(0, sign).astype(BF16)
                there = self.half.at[sign]
                send((self.name, "far", sign), self.out.at[0, sign], there, at_y(1 - 2 * sign))
            for sign in range(2):
                self.arrive(1 + sign)
                self.out[1 + sign, 1 - sign] = self.both(1 + sign, 1 - sign).astype(BF16)
                there = self.full.at[sign, 1 - sign]
                send((self.name, "full"), self.out.at[1 + sign, 1 - sign], there, at_y(1 - 2 * sign))

        def forward(self):
            for sign in range(2):
                merged = self.both(1 + sign, sign)
                receive((self.name, "far", sign), self.half.at[sign])
                self.out[1 + sign, sign] = (merged + self.half[sign].astype(F32)).astype(BF16)
                there = self.full.at[sign, sign]
                send((self.name, "full"), self.out.at[1 + sign, sign], there, at_y(1 - 2 * sign))

        def finish(self, out):
            self.arrive(3)
            own = [self.both(3, h) for h in range(2)]
            receive((self.name, "full"), self.full)
            for h in range(2):
                total = own[h] + self.full[0, h].astype(F32) + self.full[1, h].astype(F32)
                out[:, h * (D // 2) : (h + 1) * (D // 2)] = total.astype(BF16)

    class NearScatter(Scatter):
        def start(self):
            for i, step in enumerate((2, 1, 3)):
                self.arrive(i)
                for h in range(2):
                    self.out[i, h] = self.both(i, h).astype(BF16)
                send((self.name, "near"), self.out.at[i], self.full.at[i], at_y(step))

        def finish(self, out):
            self.arrive(3)
            own = [self.both(3, h) for h in range(2)]
            receive((self.name, "near"), self.full)
            for h in range(2):
                total = own[h] + self.full[0, h].astype(F32)
                total = total + self.full[1, h].astype(F32) + self.full[2, h].astype(F32)
                out[:, h * (D // 2) : (h + 1) * (D // 2)] = total.astype(BF16)

    def project_back(scatters, downs):
        down = jnp.concatenate(downs, axis=0)

        def one(i, carry):
            columns = pl.ds(pl.multiple_of(i * 512, 512), 512)
            block = nt(down, wv[columns, :])
            first = 0
            for scatter in scatters:
                count = NG * scatter.rows
                scatter.part_out(block[first : first + count], columns)
                first += count
            return carry

        lax.fori_loop(0, D // 512, one, 0)
        for scatter in scatters:
            scatter.to_core()

    q_scatter = NearScatter("Q", QR, qpart, qcore, qout, None, qfull)
    p_scatter = [
        Scatter("P%d" % h, PC, ppart.at[h], pcore.at[h], pout.at[h], phalf.at[h], pfull.at[h])
        for h in range(2)
    ]

    passage_sums(2)
    xr_start(0)
    xr_start(1)
    passage_sums(1)
    passage_sums(-1)
    xr_own(0)
    xr_own(1)
    zr_step(4)
    passage_sums(0)
    def partial_radials(a):
        column = jnp.sum(hits[a] * sum2[pl.ds(NZ + a, 1), :], axis=1, keepdims=True)
        r_out[pl.ds(a, 1)] = to_row(column, eye(GQ, SLOTS))[None]

    by_groups(partial_radials)
    r_in[pl.ds(z, 1)] = r_out[pl.ds(z, 1)]
    for s in range(1, NZ):
        send("r", r_out.at[(z + s) % NZ], r_in.at[z], at_z(s))


    total = 1.0 / to_column(inv[own_row, :], own_eye)
    inverse = 1.0 / total
    loss = jnp.log(total) + (1.0 - jnp.sum(positive * cosine, axis=1, keepdims=True)) / TEMPERATURE
    mine = (iota((GQ, SLOTS), 0) == g * QR + iota((GQ, SLOTS), 1)).astype(F32)
    loss_out[...] = jnp.sum(mine * loss, axis=0, keepdims=True)
    slope = (weight * inverse - positive) / TEMPERATURE
    pull = slope * cosine
    radial_p = jnp.sum(pull, axis=0, keepdims=True) / (square_p + EPSILON)
    coefficient = (slope / norm).astype(BF16)
    group_p = tn(coefficient, own_q)
    xr_forward(0)
    xr_forward(1)
    down_p = []
    eye_p = eye(HALF, HALF)
    for h in range(2):
        column = to_column(radial_p[:, h * HALF : (h + 1) * HALF], eye_p)
        rows = slice(h * HALF, (h + 1) * HALF)
        down_p.append(group_p[rows] - column * own_p[rows].astype(F32))
    receive("r", r_in.at[pl.ds(0, NZ - 1)])
    radials = r_in[0]
    for i in range(1, NZ):
        radials = radials + r_in[i]
    radial_slots = to_column(radials, eye_q) * inverse / TEMPERATURE
    radial_q = jnp.sum(pull, axis=1, keepdims=True) + radial_slots
    group_q = nn(coefficient, own_p) - (radial_q / (square_q + EPSILON)) * own_q32
    own_terms = query_terms(z)

    pieces = []
    for j in range(SUBS):
        piece = own_terms[j * SUB : (j + 1) * SUB]
        for sign in range(2):
            for here in (1, leap):
                receive(("zr", sign, here, j), zin.at[sign, here - 1, j])
                piece = piece + zin[sign, here - 1, j].astype(F32)
        pieces.append(piece)
    departures["zr"] = qall.at[pl.ds(0, NZ - 1)]
    factor = inverse / jnp.sqrt(square_q + EPSILON) / TEMPERATURE
    down_q = (group_q + jnp.concatenate(pieces, axis=0) * factor).astype(BF16)
    first_p = (xr_finish(0) + down_p[0]).astype(BF16)
    project_back([p_scatter[0], q_scatter], [first_p, down_q])
    second_p = (xr_finish(1) + down_p[1]).astype(BF16)
    project_back([p_scatter[1]], [second_p])
    p_scatter[0].start()
    q_scatter.start()
    p_scatter[1].start()
    p_scatter[0].forward()
    p_scatter[1].forward()
    q_scatter.finish(qg_out)
    p_scatter[0].finish(pg_out.at[0:PC])
    p_scatter[1].finish(pg_out.at[PC:PR])
    depart()
    assert not departures
    assert len(names) <= CHANNELS


def place_outputs(loss, query_grad, passage_grad, loss_out, query_out, passage_out):
    loss_out[...] = loss[0, :QR]
    query_out[...] = query_grad[...]
    passage_out[...] = passage_grad[...]


def per_device(query_hidden, passage_hidden, projection, negative_ids):
    vmem = pl.BlockSpec(memory_space=pltpu.VMEM)
    hbm = pl.BlockSpec(memory_space=pl.ANY)
    v = pltpu.VMEM
    loss, query_grad, passage_grad = pl.pallas_call(
        kernel,
        out_shape=(
            jax.ShapeDtypeStruct((1, SLOTS), F32),
            jax.ShapeDtypeStruct((QR, D), BF16),
            jax.ShapeDtypeStruct((PR, D), BF16),
        ),
        in_specs=[vmem, vmem, hbm, hbm],
        out_specs=(vmem, vmem, vmem),
        scratch_shapes=[
            v((D, COLS), BF16),
            v((NEG, NZ * NX * GQ), I32),
            v((NG, QR, D), BF16),
            v((2, NG, PC, D), BF16),
            v((NZ, GQ, COLS), BF16),
            v((NX, GP, COLS), BF16),
            v((NZ, GQ, NEG), I32),
            v((NZ, GQ, SLOTS), F32),
            v((NX, NZ, CAP, GP), BF16),
            v((NZ, SLOTS, COLS), BF16),
            v((2 * GQ, SLOTS), F32),
            v((NG, 2 * GQ, SLOTS), F32),
            v((8, SLOTS), F32),
            v((NG, 8, SLOTS), F32),
            v((1, SLOTS), F32),
            v((NZ, 1, SLOTS), F32),
            v((1, GP), F32),
            v((NX, 1, GP), F32),
            v((NZ, SLOTS), F32),
            v((NZ, SLOTS), F32),
            v((NZ, SLOTS), F32),
            v((NG, NZ, SLOTS), F32),
            v((2 * NZ, SLOTS), F32),
            v((NZ, SLOTS), F32),
            v((NZ, SLOTS), F32),
            v((NZ, SLOTS), F32),
            v((NZ, SLOTS), F32),
            v((NZ // 2, SLOTS), F32),
            v((NZ, NZ // 2, SLOTS), F32),
            v((NZ // 2, SLOTS), F32),
            v((NZ, 1, SLOTS), F32),
            v((NZ, 1, SLOTS), F32),
            v((2, NZ // 2, SUBS, SUB, COLS), BF16),
            v((2, NZ // 2, SUBS, SUB, COLS), BF16),
            v((NZ, SLOTS, GQ), BF16),
            v((NX, GP, NZ * CAP), BF16),
            v((NX, NZ, CAP, COLS), BF16),
            v((NX, GP, COLS), F32),
            v((2, 3, 2, HALF // 2, COLS), BF16),
            v((2, 2, HALF // 2, COLS), BF16),
            v((2, 2, 2, HALF // 2, COLS), BF16),
            v((NC, NY, QR, D), BF16),
            v((NY, QR, D), BF16),
            v((3, 2, QR, D // 2), BF16),
            v((3, 2, QR, D // 2), BF16),
            v((2, NC, NY, PC, D), BF16),
            v((2, NY, PC, D), BF16),
            v((2, 3, 2, PC, D // 2), BF16),
            v((2, 2, PC, D // 2), BF16),
            v((2, 2, 2, PC, D // 2), BF16),
            pltpu.SemaphoreType.DMA((10,)),
            pltpu.SemaphoreType.DMA((CHANNELS,)),
            pltpu.SemaphoreType.DMA((CHANNELS,)),
        ],
        compiler_params=pltpu.CompilerParams(
            collective_id=0, has_side_effects=True, vmem_limit_bytes=56 * 1024 * 1024
        ),
    )(query_hidden, passage_hidden, projection, negative_ids.T)
    return pl.pallas_call(
        place_outputs,
        out_shape=(
            jax.ShapeDtypeStruct((QR,), F32),
            jax.ShapeDtypeStruct((QR, D), BF16),
            jax.ShapeDtypeStruct((PR, D), BF16),
        ),
        in_specs=[vmem, vmem, vmem],
        out_specs=(vmem, vmem, vmem),
    )(loss, query_grad, passage_grad)


def solution(mesh):
    in_specs = (P(("dp", "group"), None), P(("dp", "group"), None), P(None, "group"), P())
    out_specs = (P(("dp", "group")), P(("dp", "group"), None), P(("dp", "group"), None))
    return jax.shard_map(
        per_device, mesh=mesh, in_specs=in_specs, out_specs=out_specs, check_vma=False
    )
```

```python
import jax
import jax.numpy as jnp
from jax import lax
from jax.experimental import pallas as pl
from jax.experimental.pallas import tpu as pltpu
from jax.sharding import PartitionSpec as P

TEMPERATURE = 0.05
EPSILON = 1e-06
MESH = pl.DeviceIdType.MESH
F32, BF16, I32 = jnp.float32, jnp.bfloat16, jnp.int32

NZ, NX, NY, NC = 16, 4, 4, 2
NG = NY * NC
D = 4096
COLS = D // NG
QR, PR, PC = 8, 32, 16
GQ, GP = QR * NG, PR * NG
HALF = GP // 2
NEG, CAP = 16, 32
SLOTS = NX * CAP
CHANNELS = 256
SUBS = 2
SUB = GQ // SUBS


def nn(a, b):
    return lax.dot_general(a, b, (((1,), (0,)), ((), ())), preferred_element_type=F32)


def nt(a, b):
    return lax.dot_general(a, b, (((1,), (1,)), ((), ())), preferred_element_type=F32)


def tn(a, b):
    return lax.dot_general(a, b, (((0,), (0,)), ((), ())), preferred_element_type=F32)


def iota(shape, dim):
    return lax.broadcasted_iota(I32, shape, dim)


def eye(rows, columns):
    return (iota((rows, columns), 0) == iota((rows, columns), 1)).astype(F32)


def to_row(column, identity):
    return jnp.sum(identity * column, axis=0, keepdims=True)


def to_column(row, identity):
    return jnp.sum(identity * row, axis=1, keepdims=True)


def kernel(
    qh, ph, weight_hbm, ids_hbm,
    loss_out, qg_out, pg_out,
    wv, idv, hq, hp, qall, pall, code, hits, one_hot, prow,
    pay1, got1, payn, gotn, nz_out, nz_in, nx_out, nx_in, sl_q, sl_p,
    pay2, got2, sum2, fill, w_p, k_c, r_c, t_out, t_in, inv, r_out, r_in,
    zout, zin, turned_k, turned_hot, cq, gp, xout, xhalf, xfull,
    qpart, qcore, qout, qfull, ppart, pcore, pout, phalf, pfull,
    local_sem, send_sem, recv_sem,
):
    dp, g = lax.axis_index("dp"), lax.axis_index("group")
    z, x = dp // NX, dp % NX
    y, c = g // NC, g % NC

    def at_z(step):
        return (((z + step + 2 * NZ) % NZ) * NX + x, g)

    def at_x(step):
        return (z * NX + (x + step + NX) % NX, g)

    def member(step, other):
        return ((y + step + NY) % NY) * NC + (1 - c if other else c)

    def at_y(step, other=False):
        return (dp, member(step, other))

    others = [(s, o) for s in (0, 1, 2, 3) for o in (False, True) if (s, o) != (0, False)]

    names, departures = {}, {}

    def channel(name):
        return names.setdefault(name, len(names))

    def copy(name, group, src, dst, device):
        return pltpu.make_async_remote_copy(
            src_ref=src, dst_ref=dst, send_sem=send_sem.at[channel(("from", group))],
            recv_sem=recv_sem.at[channel(name)], device_id=device, device_id_type=MESH,
        )

    def send(name, src, dst, device, group=None):
        group = name if group is None else group
        departures.setdefault(group, None)
        copy(name, group, src, dst, device).start()

    def receive(name, dst):
        if name in departures:
            departures[name] = dst
        copy(name, name, dst, dst, at_x(1)).wait_recv()

    def depart():
        for group, ref in list(departures.items()):
            if ref is not None:
                copy(group, group, ref, ref, at_x(1)).wait_send()
                del departures[group]

    w_copies = []
    for k in range(8):
        rows = pl.ds(k * COLS, COLS)
        w_copies.append(pltpu.make_async_copy(weight_hbm.at[rows], wv.at[rows], local_sem.at[2 + k]))
        w_copies[-1].start()
    id_copy = pltpu.make_async_copy(ids_hbm, idv, local_sem.at[1])
    id_copy.start()
    barrier = pltpu.get_barrier_semaphore()
    greeted = [at_z(s) for s in range(1, NZ)] + [at_x(s) for s in range(1, NX)] + [at_y(*o) for o in others]
    for device in greeted:
        pl.semaphore_signal(barrier, inc=1, device_id=device, device_id_type=MESH)
    pl.semaphore_wait(barrier, len(greeted))

    def columns(h):
        return pl.ds(h * (D // 2), D // 2)

    class Gather:
        def __init__(self, name, src, held):
            self.name, self.src, self.held = name, src, held

        def start(self):
            for k in range(2):
                for sign, step in ((0, 1), (1, -1)):
                    h = k if sign == 0 else 1 - k
                    here = self.held.at[g, :, columns(h)]
                    send((self.name, sign, h), self.src.at[:, columns(h)], here, at_y(step))
            send((self.name, "c"), self.src, self.held.at[g], at_y(0, True))
            self.held[pl.ds(g, 1)] = self.src[...][None]

        def forward(self):
            for k in range(2):
                for sign, step in ((0, 1), (1, -1)):
                    h = k if sign == 0 else 1 - k
                    block = member(-step, False)
                    piece = self.held.at[block, :, columns(h)]
                    receive((self.name, sign, h), piece)
                    if k == 0:
                        send((self.name, "far"), piece, piece, at_y(step))
                    else:
                        whole = self.held.at[block]
                        send((self.name, "c"), whole, whole, at_y(0, True))

        def forward_far(self):
            whole = self.held.at[member(2, False)]
            receive((self.name, "far"), whole)
            send((self.name, "c"), whole, whole, at_y(0, True))

        def finish(self):
            receive((self.name, "c"), self.held.at[pl.ds(0, NY)])

    class Near:
        def __init__(self, name, src, held):
            self.name, self.src, self.held = name, src, held

        def start(self):
            for step in (2, 1, 3):
                send((self.name, step), self.src, self.held.at[g], at_y(step))
            send((self.name, "c"), self.src, self.held.at[g], at_y(0, True))
            self.held[pl.ds(g, 1)] = self.src[...][None]

        def forward(self):
            for step in (1, 3, 2):
                block = self.held.at[member(-step, False)]
                receive((self.name, step), block)
                send((self.name, "c"), block, block, at_y(0, True))

        def finish(self):
            receive((self.name, "c"), self.held.at[pl.ds(0, NY)])

    q_gather = Near("q", qh, hq)
    p_gather = [Gather("p%d" % h, ph.at[pl.ds(h * PC, PC)], hp.at[h]) for h in range(2)]

    far = NZ // 2
    leap = far // 2

    def halved(sign):
        return range(sign * SUBS // 2, (sign + 1) * SUBS // 2)

    def z_piece(sign, distance, j):
        block = (z - (1 - 2 * sign) * distance + 2 * NZ) % NZ
        return qall.at[block, pl.ds(j * SUB, SUB)]

    def z_hop(here, there):
        for j in range(SUBS):
            for sign in range(2):
                if there < far or j in halved(sign):
                    piece = z_piece(sign, here, j)
                    if here > 0:
                        receive(("z", sign, here, j), piece)
                    target = at_z((1 - 2 * sign) * (there - here))
                    send(("z", sign, there, j), piece, piece, target, "z")

    def z_step(s):
        if s == 0:
            z_hop(0, 1)
            z_hop(0, leap)
        else:
            if s + 1 < leap:
                z_hop(s, s + 1)
            z_hop(leap + s - 1, leap + s)
        if s == leap:
            for j in range(SUBS):
                for sign in range(2):
                    receive(("z", sign, leap - 1, j), z_piece(sign, leap - 1, j))

    def z_finish():
        for j in range(SUBS):
            for sign in range(2):
                distance = far if j in halved(sign) else far - 1
                receive(("z", sign, distance, j), z_piece(sign, distance, j))
        departures["z"] = qall.at[pl.ds(0, NZ - 1)]

    def x_piece(block, h, half):
        return pall.at[block, pl.ds(h * HALF + half * (HALF // 2), HALF // 2)]

    def x_start(h):
        for k in range(2):
            for sign in range(2):
                half = k if sign == 0 else 1 - k
                piece = x_piece(x, h, half)
                send(("x", h, sign, half), piece, piece, at_x(1 - 2 * sign))

    def x_forward(h):
        for sign in range(2):
            step = 1 - 2 * sign
            piece = x_piece((x - step + NX) % NX, h, sign)
            receive(("x", h, sign, sign), piece)
            send(("x", h, "far"), piece, piece, at_x(step))

    def x_finish(h):
        for sign in range(2):
            step = 1 - 2 * sign
            receive(("x", h, sign, 1 - sign), x_piece((x - step + NX) % NX, h, 1 - sign))
        receive(("x", h, "far"), pall.at[(x + 2) % NX, pl.ds(h * HALF, HALF)])

    def find_slots():
        pieces = []
        for a in range(NZ):
            start = pl.multiple_of(a * NX * GQ + (x // 2) * 2 * GQ, 2 * GQ)
            pieces.append(idv[:, pl.ds(start, 2 * GQ)].astype(F32))
        turned = jnp.concatenate(pieces, axis=0).T
        odd = (x % 2).astype(F32)
        ids = (turned[:GQ] * (1.0 - odd) + turned[GQ:] * odd).astype(I32)
        owner = (ids >> 8) - z * NX
        place = ids & 255
        place = ((place >> 4) & 1) * HALF + (place >> 5) * PC + (place & 15)
        mine = jnp.concatenate([(owner == o).astype(F32) for o in range(NX)], axis=0)
        picked = mine.astype(BF16)
        shape = (NX * GQ, NZ * NEG)
        i, j = iota(shape, 0), iota(shape, 1)
        before = ((i // GQ == j // GQ) & (j < i)).astype(F32).astype(BF16)
        same = i // NEG == j // NEG
        ahead = (same & (i < j)).astype(F32).astype(BF16)
        row_sums = nn(before, picked).astype(BF16)
        rank = nn(row_sums, same.astype(F32).astype(BF16)) + nn(picked, ahead)
        slot = mine * (rank + ((i // GQ) * CAP + 1).astype(F32))
        slot = slot[:GQ] + slot[GQ : 2 * GQ] + slot[2 * GQ : 3 * GQ] + slot[3 * GQ :]
        both = slot.astype(I32) * 256 + place
        both = jnp.where(slot > 0.0, both, 0)
        for a in range(NZ):
            code[a] = both[:, a * NEG : (a + 1) * NEG]

    def fill_slots(first, count):
        def one(a, carry):
            block = code[a]
            lane = iota((GQ, SLOTS), 1) + 1
            hit = jnp.zeros((GQ, SLOTS), F32)
            spot = jnp.zeros((GQ, SLOTS), I32)
            for k in range(NEG):
                column = jnp.broadcast_to(block[:, k : k + 1], (GQ, SLOTS))
                found = (column >> 8) == lane
                hit = jnp.where(found, 1.0, hit)
                spot = jnp.where(found, column & 255, spot)
            hits[a] = hit
            fill[pl.ds(a, 1), :] = jnp.sum(hit, axis=0, keepdims=True)
            row = jnp.sum(spot.astype(F32), axis=0, keepdims=True)
            column = to_column(row, eye(SLOTS, SLOTS)).astype(I32)
            chosen = (iota((SLOTS, GP), 1) == column).astype(F32).astype(BF16)
            for o in range(NX):
                one_hot[o, a] = chosen[o * CAP : (o + 1) * CAP]
            return carry

        def two(i, carry):
            one(first + 2 * i, carry)
            return one(first + 2 * i + 1, carry)

        lax.fori_loop(0, count // 2, two, 0)

    def share(name, pay, got):
        for step, other in others:
            send(name, pay, got.at[g], at_y(step, other))

    def collect(name, pay, got):
        got[pl.ds(g, 1)] = pay[...][None]
        receive(name, got.at[pl.ds(0, NG - 1)])
        total = got[0]
        for i in range(1, NG):
            total = total + got[i]
        return total

    def project_passages(h):
        rows = hp[h].reshape(HALF, D)
        pall[pl.ds(x, 1), h * HALF : (h + 1) * HALF] = nn(rows, wv[...]).astype(BF16)[None]
        x_start(h)

    eye_q, eye_s = eye(GQ, SLOTS), eye(SLOTS, SLOTS)
    p_first, p_second = p_gather

    q_gather.start()
    p_first.start()
    p_second.start()
    id_copy.wait()
    find_slots()
    q_gather.forward()
    fill_slots(0, 4)
    p_first.forward()
    q_gather.finish()
    rows = hq[...].astype(F32).reshape(GQ, D).astype(BF16)
    projected = jnp.zeros((GQ, COLS), F32)
    for k, one in enumerate(w_copies):
        one.wait()
        part = slice(k * COLS, (k + 1) * COLS)
        projected = projected + nn(rows[:, part], wv[part, :])
    qall[pl.ds(z, 1)] = projected.astype(BF16)[None]
    z_step(0)
    p_second.forward()
    p_first.forward_far()
    fill_slots(4, 4)
    p_first.finish()
    project_passages(0)
    z_step(1)
    p_second.forward_far()
    fill_slots(8, 2)
    p_second.finish()
    project_passages(1)
    z_step(2)

    own_q, own_p = qall[z], pall[x]
    for h in range(2):
        part = own_p[h * HALF : (h + 1) * HALF]
        payn[h : h + 1] = jnp.sum(nt(part, part) * eye_s, axis=0, keepdims=True)
    own_q32 = own_q.astype(F32)
    payn[2:3] = to_row(jnp.sum(own_q32 * own_q32, axis=1, keepdims=True), eye_q)
    payn[3:] = jnp.zeros((payn.shape[0] - 3, SLOTS), F32)
    share("n", payn, gotn)

    inner = nt(own_q, own_p)
    pay1[0:GQ] = inner[:, :SLOTS]
    pay1[GQ:] = inner[:, SLOTS:]
    share("s1", pay1, got1)
    x_forward(0)
    z_step(3)
    fill_slots(10, 4)
    sums = collect("n", payn, gotn)
    square_p = jnp.concatenate([sums[0:1], sums[1:2]], axis=1)
    square_q = to_column(sums[2:3], eye_q)
    nz_out[...] = sums[2:3]
    nx_out[...] = square_p
    nz_in[pl.ds(z, 1)] = sums[2:3][None]
    nx_in[pl.ds(x, 1)] = square_p[None]
    for s in range(1, NX):
        send("nx", nx_out, nx_in.at[x], at_x(s))
    for s in range(1, NZ):
        send("nz", nz_out, nz_in.at[z], at_z(s))
    x_forward(1)
    z_step(4)
    fill_slots(14, 2)
    x_finish(0)
    x_finish(1)

    for o in range(NX):
        chosen = nn(one_hot[o].reshape(NZ * CAP, GP), pall[o])
        prow[:, o * CAP : (o + 1) * CAP, :] = chosen.astype(BF16).reshape(NZ, CAP, COLS)

    def by_groups(one, first=0, count=NZ, width=8):
        def some(i, carry):
            for k in range(width):
                one(first + i * width + k)
            return carry

        lax.fori_loop(0, count // width, some, 0)

    def pair_products(step):
        a = (z + step + 2 * NZ) % NZ
        products = nt(qall[a], prow[a])
        pay2[pl.ds(a, 1), :] = jnp.sum(products * hits[a], axis=0, keepdims=True)

    by_groups(pair_products, 2 - NZ // 2, NZ - 4, 6)
    z_finish()
    for step in (NZ // 2 - 2, NZ // 2 - 1, NZ // 2, NZ // 2 + 1):
        pair_products(step)
    share("s2", pay2, got2)

    receive("nx", nx_in.at[pl.ds(0, NX - 1)])
    receive("nz", nz_in.at[pl.ds(0, NZ - 1)])

    depart()

    def slot_norms(a):
        column = to_column(nz_in[a], eye(GQ, SLOTS))
        sl_q[pl.ds(a, 1), :] = jnp.sum(hits[a] * column, axis=0, keepdims=True)
        columns = [
            jnp.sum(one_hot[o, a].astype(F32) * nx_in[o], axis=1, keepdims=True) for o in range(NX)
        ]
        sl_p[pl.ds(a, 1), :] = to_row(jnp.concatenate(columns, axis=0), eye(SLOTS, SLOTS))

    by_groups(slot_norms)

    sums = collect("s1", pay1, got1)
    inner = jnp.concatenate([sums[0:GQ], sums[GQ : 2 * GQ]], axis=1)
    norm = jnp.sqrt(square_q + EPSILON) * jnp.sqrt(square_p + EPSILON)
    cosine = inner / norm
    weight = jnp.exp((cosine - 1.0) / TEMPERATURE)
    weight_sum = jnp.sum(weight, axis=1, keepdims=True)
    spot = iota((GQ, GP), 1)
    passage = ((spot >> 4) & 7) * PR + (spot >> 7) * PC + (spot & 15)
    positive = (passage == iota((GQ, GP), 0) * 4).astype(F32)

    inner_slot = collect("s2", pay2, got2)
    square_slot_p = sl_p[...]
    norm_slot_q = jnp.sqrt(sl_q[...] + EPSILON)
    norm_slot_p = jnp.sqrt(square_slot_p + EPSILON)
    cosine_slot = inner_slot / (norm_slot_q * norm_slot_p)
    weight_slot = jnp.exp((cosine_slot - 1.0) / TEMPERATURE) * fill[...]
    sum2[0:NZ] = weight_slot
    sum2[NZ:] = weight_slot * cosine_slot
    w_p[...] = weight_slot / norm_slot_p
    k_c[...] = weight_slot / (norm_slot_q * norm_slot_p) / TEMPERATURE
    r_c[...] = weight_slot * cosine_slot / (square_slot_p + EPSILON) / TEMPERATURE

    def query_terms(a):
        coefficient = (hits[a] * w_p[pl.ds(a, 1), :]).astype(BF16)
        return nn(coefficient, prow[a])

    def zr_hop(here, there):
        terms = None
        for sign in range(2):
            step = 1 - 2 * sign
            if here < far or terms is None:
                terms = query_terms((z + step * here + NZ) % NZ)
            for j in range(SUBS):
                if here == far and j not in halved(sign):
                    continue
                value = terms[j * SUB : (j + 1) * SUB]
                if here not in (far, leap - 1) and (here < far - 1 or j in halved(sign)):
                    receive(("zr", sign, here + 1, j), zin.at[sign, here, j])
                    value = value + zin[sign, here, j].astype(F32)
                zout[sign, here - 1, j] = value.astype(BF16)
                target = zin.at[sign, here - 1, j]
                send(("zr", sign, here, j), zout.at[sign, here - 1, j], target, at_z(step * (here - there)), "zr")

    def zr_step(s):
        here = far - s
        zr_hop(here, here - 1 if here > leap else 0)
        if s < leap - 1:
            zr_hop(leap - 1 - s, leap - 2 - s)

    def eye_at(second):
        return (iota((GQ, SLOTS), 1) == iota((GQ, SLOTS), 0) + GQ * second).astype(F32)

    def partial_totals(i):
        row = jnp.zeros((1, SLOTS), F32)
        for second in range(2):
            a = i + second * (NZ // 2)
            column = jnp.sum(hits[a] * sum2[pl.ds(a, 1), :], axis=1, keepdims=True)
            row = row + to_row(column, eye_at(second))
        t_out[pl.ds(i, 1), :] = row

    by_groups(partial_totals, 0, NZ // 2)
    own_row, own_eye = pl.ds(z % (NZ // 2), 1), eye_at(z // (NZ // 2))
    t_out[own_row, :] = t_out[own_row, :] + to_row(weight_sum, own_eye)
    t_in[pl.ds(z, 1)] = t_out[...][None]
    for s in range(1, NZ):
        send("t", t_out, t_in.at[z], at_z(s))
    zr_step(0)

    def turn_terms(a):
        turned_k[a] = (hits[a] * k_c[pl.ds(a, 1), :]).T.astype(BF16)

    by_groups(turn_terms)
    zr_step(1)
    for o in range(NX):
        turned_hot[o] = one_hot[o].reshape(NZ * CAP, GP).astype(F32).T.astype(BF16)

    receive("t", t_in.at[pl.ds(0, NZ - 1)])
    totals = t_in[0]
    for i in range(1, NZ):
        totals = totals + t_in[i]
    inv[...] = 1.0 / totals

    def passage_terms(a):
        column = to_column(inv[pl.ds(a % (NZ // 2), 1), :], eye_at(a // (NZ // 2)))
        scaled = (qall[a].astype(F32) * column).astype(BF16)
        shares = jnp.sum(hits[a] * column, axis=0, keepdims=True) * r_c[pl.ds(a, 1), :]
        pulls = (eye(SLOTS, SLOTS) * (-shares)).astype(BF16)
        lhs = jnp.concatenate([pulls, turned_k[a]], axis=1)
        terms = nn(lhs, jnp.concatenate([prow[a], scaled], axis=0)).astype(BF16)
        for o in range(NX):
            cq[o, a] = terms[o * CAP : (o + 1) * CAP]

    by_groups(passage_terms, 0, NZ // 2)
    zr_step(2)
    by_groups(passage_terms, NZ // 2, NZ // 2)
    zr_step(3)

    def passage_sums(step):
        o = (x + step + NX) % NX
        gp[o] = nn(turned_hot[o], cq[o].reshape(NZ * CAP, COLS))

    def xr_rows(h, half):
        return slice(h * HALF + half * (HALF // 2), h * HALF + (half + 1) * (HALF // 2))

    def xr_start(h):
        for sign in range(2):
            xout[h, 0, sign] = gp[(x + 2) % NX, xr_rows(h, sign)].astype(BF16)
            send(("xr", h, sign, "far"), xout.at[h, 0, sign], xhalf.at[h, sign], at_x(1 - 2 * sign))

    def xr_own(h):
        for sign in range(2):
            near = (x + 1 - 2 * sign + NX) % NX
            xout[h, 1 + sign, 1 - sign] = gp[near, xr_rows(h, 1 - sign)].astype(BF16)
            there = xfull.at[h, sign, 1 - sign]
            send(("xr", h), xout.at[h, 1 + sign, 1 - sign], there, at_x(1 - 2 * sign))

    def xr_forward(h):
        for sign in range(2):
            near = (x + 1 - 2 * sign + NX) % NX
            receive(("xr", h, sign, "far"), xhalf.at[h, sign])
            merged = gp[near, xr_rows(h, sign)] + xhalf[h, sign].astype(F32)
            xout[h, 1 + sign, sign] = merged.astype(BF16)
            there = xfull.at[h, sign, sign]
            send(("xr", h), xout.at[h, 1 + sign, sign], there, at_x(1 - 2 * sign))

    def xr_finish(h):
        receive(("xr", h), xfull.at[h])
        value = gp[x, h * HALF : (h + 1) * HALF]
        full = xfull[h].reshape(2, HALF, COLS)
        return value + full[0].astype(F32) + full[1].astype(F32)

    class Scatter:
        def __init__(self, name, rows, part, core, out, half, full):
            self.name, self.rows = name, rows
            self.part, self.core, self.out, self.half, self.full = part, core, out, half, full
            self.places = [(y + step) % NY for step in (2, 1, 3, 0)]

        def part_out(self, block, columns):
            block = block.reshape(NY, NC, self.rows, 512)
            for k in range(NC):
                self.part[k, :, :, columns] = block[:, k].astype(BF16)

        def to_core(self):
            for i, place in enumerate(self.places):
                there = self.core.at[place]
                send((self.name, "c", i), self.part.at[1 - c, place], there, at_y(0, True))

        def arrive(self, i):
            receive((self.name, "c", i), self.core.at[self.places[i]])

        def both(self, i, h):
            place = self.places[i]
            cut = slice(h * (D // 2), (h + 1) * (D // 2))
            return self.part[c, place, :, cut].astype(F32) + self.core[place, :, cut].astype(F32)

        def start(self):
            self.arrive(0)
            for sign in range(2):
                self.out[0, sign] = self.both(0, sign).astype(BF16)
                there = self.half.at[sign]
                send((self.name, "far", sign), self.out.at[0, sign], there, at_y(1 - 2 * sign))
            for sign in range(2):
                self.arrive(1 + sign)
                self.out[1 + sign, 1 - sign] = self.both(1 + sign, 1 - sign).astype(BF16)
                there = self.full.at[sign, 1 - sign]
                send((self.name, "full"), self.out.at[1 + sign, 1 - sign], there, at_y(1 - 2 * sign))

        def forward(self):
            for sign in range(2):
                merged = self.both(1 + sign, sign)
                receive((self.name, "far", sign), self.half.at[sign])
                self.out[1 + sign, sign] = (merged + self.half[sign].astype(F32)).astype(BF16)
                there = self.full.at[sign, sign]
                send((self.name, "full"), self.out.at[1 + sign, sign], there, at_y(1 - 2 * sign))

        def finish(self, out):
            self.arrive(3)
            own = [self.both(3, h) for h in range(2)]
            receive((self.name, "full"), self.full)
            for h in range(2):
                total = own[h] + self.full[0, h].astype(F32) + self.full[1, h].astype(F32)
                out[:, h * (D // 2) : (h + 1) * (D // 2)] = total.astype(BF16)

    class NearScatter(Scatter):
        def start(self):
            for i, step in enumerate((2, 1, 3)):
                self.arrive(i)
                for h in range(2):
                    self.out[i, h] = self.both(i, h).astype(BF16)
                send((self.name, "near"), self.out.at[i], self.full.at[i], at_y(step))

        def finish(self, out):
            self.arrive(3)
            own = [self.both(3, h) for h in range(2)]
            receive((self.name, "near"), self.full)
            for h in range(2):
                total = own[h] + self.full[0, h].astype(F32)
                total = total + self.full[1, h].astype(F32) + self.full[2, h].astype(F32)
                out[:, h * (D // 2) : (h + 1) * (D // 2)] = total.astype(BF16)

    def project_back(scatters, downs):
        down = jnp.concatenate(downs, axis=0)

        def one(i, carry):
            columns = pl.ds(pl.multiple_of(i * 512, 512), 512)
            block = nt(down, wv[columns, :])
            first = 0
            for scatter in scatters:
                count = NG * scatter.rows
                scatter.part_out(block[first : first + count], columns)
                first += count
            return carry

        lax.fori_loop(0, D // 512, one, 0)
        for scatter in scatters:
            scatter.to_core()

    q_scatter = NearScatter("Q", QR, qpart, qcore, qout, None, qfull)
    p_scatter = [
        Scatter("P%d" % h, PC, ppart.at[h], pcore.at[h], pout.at[h], phalf.at[h], pfull.at[h])
        for h in range(2)
    ]

    passage_sums(2)
    xr_start(0)
    xr_start(1)
    passage_sums(1)
    passage_sums(-1)
    xr_own(0)
    xr_own(1)
    zr_step(4)
    passage_sums(0)
    def partial_radials(a):
        column = jnp.sum(hits[a] * sum2[pl.ds(NZ + a, 1), :], axis=1, keepdims=True)
        r_out[pl.ds(a, 1)] = to_row(column, eye(GQ, SLOTS))[None]

    by_groups(partial_radials)
    r_in[pl.ds(z, 1)] = r_out[pl.ds(z, 1)]
    for s in range(1, NZ):
        send("r", r_out.at[(z + s) % NZ], r_in.at[z], at_z(s))


    total = 1.0 / to_column(inv[own_row, :], own_eye)
    inverse = 1.0 / total
    loss = jnp.log(total) + (1.0 - jnp.sum(positive * cosine, axis=1, keepdims=True)) / TEMPERATURE
    mine = (iota((GQ, SLOTS), 0) == g * QR + iota((GQ, SLOTS), 1)).astype(F32)
    loss_out[...] = jnp.sum(mine * loss, axis=0, keepdims=True)
    slope = (weight * inverse - positive) / TEMPERATURE
    pull = slope * cosine
    radial_p = jnp.sum(pull, axis=0, keepdims=True) / (square_p + EPSILON)
    coefficient = (slope / norm).astype(BF16)
    group_p = tn(coefficient, own_q)
    xr_forward(0)
    xr_forward(1)
    down_p = []
    eye_p = eye(HALF, HALF)
    for h in range(2):
        column = to_column(radial_p[:, h * HALF : (h + 1) * HALF], eye_p)
        rows = slice(h * HALF, (h + 1) * HALF)
        down_p.append(group_p[rows] - column * own_p[rows].astype(F32))
    receive("r", r_in.at[pl.ds(0, NZ - 1)])
    radials = r_in[0]
    for i in range(1, NZ):
        radials = radials + r_in[i]
    radial_slots = to_column(radials, eye_q) * inverse / TEMPERATURE
    radial_q = jnp.sum(pull, axis=1, keepdims=True) + radial_slots
    group_q = nn(coefficient, own_p) - (radial_q / (square_q + EPSILON)) * own_q32
    own_terms = query_terms(z)

    pieces = []
    for j in range(SUBS):
        piece = own_terms[j * SUB : (j + 1) * SUB]
        for sign in range(2):
            for here in (1, leap):
                receive(("zr", sign, here, j), zin.at[sign, here - 1, j])
                piece = piece + zin[sign, here - 1, j].astype(F32)
        pieces.append(piece)
    departures["zr"] = qall.at[pl.ds(0, NZ - 1)]
    factor = inverse / jnp.sqrt(square_q + EPSILON) / TEMPERATURE
    down_q = (group_q + jnp.concatenate(pieces, axis=0) * factor).astype(BF16)
    first_p = (xr_finish(0) + down_p[0]).astype(BF16)
    project_back([p_scatter[0], q_scatter], [first_p, down_q])
    second_p = (xr_finish(1) + down_p[1]).astype(BF16)
    project_back([p_scatter[1]], [second_p])
    p_scatter[0].start()
    q_scatter.start()
    p_scatter[1].start()
    p_scatter[0].forward()
    p_scatter[1].forward()
    q_scatter.finish(qg_out)
    p_scatter[0].finish(pg_out.at[0:PC])
    p_scatter[1].finish(pg_out.at[PC:PR])
    depart()
    assert not departures
    assert len(names) <= CHANNELS


def place_outputs(loss, query_grad, passage_grad, loss_out, query_out, passage_out):
    loss_out[...] = loss[0, :QR]
    query_out[...] = query_grad[...]
    passage_out[...] = passage_grad[...]


def per_device(query_hidden, passage_hidden, projection, negative_ids):
    vmem = pl.BlockSpec(memory_space=pltpu.VMEM)
    hbm = pl.BlockSpec(memory_space=pl.ANY)
    v = pltpu.VMEM
    loss, query_grad, passage_grad = pl.pallas_call(
        kernel,
        out_shape=(
            jax.ShapeDtypeStruct((1, SLOTS), F32),
            jax.ShapeDtypeStruct((QR, D), BF16),
            jax.ShapeDtypeStruct((PR, D), BF16),
        ),
        in_specs=[vmem, vmem, hbm, hbm],
        out_specs=(vmem, vmem, vmem),
        scratch_shapes=[
            v((D, COLS), BF16),
            v((NEG, NZ * NX * GQ), I32),
            v((NG, QR, D), BF16),
            v((2, NG, PC, D), BF16),
            v((NZ, GQ, COLS), BF16),
            v((NX, GP, COLS), BF16),
            v((NZ, GQ, NEG), I32),
            v((NZ, GQ, SLOTS), F32),
            v((NX, NZ, CAP, GP), BF16),
            v((NZ, SLOTS, COLS), BF16),
            v((2 * GQ, SLOTS), F32),
            v((NG, 2 * GQ, SLOTS), F32),
            v((8, SLOTS), F32),
            v((NG, 8, SLOTS), F32),
            v((1, SLOTS), F32),
            v((NZ, 1, SLOTS), F32),
            v((1, GP), F32),
            v((NX, 1, GP), F32),
            v((NZ, SLOTS), F32),
            v((NZ, SLOTS), F32),
            v((NZ, SLOTS), F32),
            v((NG, NZ, SLOTS), F32),
            v((2 * NZ, SLOTS), F32),
            v((NZ, SLOTS), F32),
            v((NZ, SLOTS), F32),
            v((NZ, SLOTS), F32),
            v((NZ, SLOTS), F32),
            v((NZ // 2, SLOTS), F32),
            v((NZ, NZ // 2, SLOTS), F32),
            v((NZ // 2, SLOTS), F32),
            v((NZ, 1, SLOTS), F32),
            v((NZ, 1, SLOTS), F32),
            v((2, NZ // 2, SUBS, SUB, COLS), BF16),
            v((2, NZ // 2, SUBS, SUB, COLS), BF16),
            v((NZ, SLOTS, GQ), BF16),
            v((NX, GP, NZ * CAP), BF16),
            v((NX, NZ, CAP, COLS), BF16),
            v((NX, GP, COLS), F32),
            v((2, 3, 2, HALF // 2, COLS), BF16),
            v((2, 2, HALF // 2, COLS), BF16),
            v((2, 2, 2, HALF // 2, COLS), BF16),
            v((NC, NY, QR, D), BF16),
            v((NY, QR, D), BF16),
            v((3, 2, QR, D // 2), BF16),
            v((3, 2, QR, D // 2), BF16),
            v((2, NC, NY, PC, D), BF16),
            v((2, NY, PC, D), BF16),
            v((2, 3, 2, PC, D // 2), BF16),
            v((2, 2, PC, D // 2), BF16),
            v((2, 2, 2, PC, D // 2), BF16),
            pltpu.SemaphoreType.DMA((10,)),
            pltpu.SemaphoreType.DMA((CHANNELS,)),
            pltpu.SemaphoreType.DMA((CHANNELS,)),
        ],
        compiler_params=pltpu.CompilerParams(
            collective_id=0, has_side_effects=True, vmem_limit_bytes=56 * 1024 * 1024
        ),
    )(query_hidden, passage_hidden, projection, negative_ids.T)
    return pl.pallas_call(
        place_outputs,
        out_shape=(
            jax.ShapeDtypeStruct((QR,), F32),
            jax.ShapeDtypeStruct((QR, D), BF16),
            jax.ShapeDtypeStruct((PR, D), BF16),
        ),
        in_specs=[vmem, vmem, vmem],
        out_specs=(vmem, vmem, vmem),
    )(loss, query_grad, passage_grad)


def solution(mesh):
    in_specs = (P(("dp", "group"), None), P(("dp", "group"), None), P(None, "group"), P())
    out_specs = (P(("dp", "group")), P(("dp", "group"), None), P(("dp", "group"), None))
    return jax.shard_map(
        per_device, mesh=mesh, in_specs=in_specs, out_specs=out_specs, check_vma=False
    )
```
